32 devices in a mesh: dp: 8 (over y, x, core), mp: 4 (over z).
Axes of the slice: x: 2, y: 2, z: 4, core: 2. Of those that a mesh axis runs over, the one named last changes fastest.
Arguments:
- queries: bfloat16 [128, 2048], P('dp', 'mp'), may hold values from -160 to 160
- prefix_pool: bfloat16 [48, 2, 2, 128, 128], P('dp'), may hold values from -6 to 6
- slot_offset: int32 [48], P('dp'), may hold values from 0 to 5, as said below
- suffix_kv: bfloat16 [128, 2, 2, 48, 128], P('dp'), may hold values from -7.1875 to 7.1875
- out_weight: bfloat16 [2048, 8192], P('mp'), may hold values from -0.125 to 0.125
Outputs:
- block_out: bfloat16 [128, 8192], P('dp')
The draws below stay inside these ranges and needn't reach their ends.
Inputs may be any that keep to these rules, and one draw needn't show every extreme that they name: `slot_offset`: on every index of dp, among its 6 blocks no value occurs more than 2 times and some value occurs exactly 2 times. One document gets at most 12 blocks, and in every draw some document gets that many.
All inputs are finite; a program needn't handle non-finite values.
Results may differ from the reference program's by a relative error of at most 0.023.
Values may be sent and summed in bfloat16 or wider, within the bound.
No kernel may reach another device: no remote copies, remote signals or barrier semaphores. Data moves between devices by JAX's collectives and lax.ppermute only.
A program may use at most 64 MiB of HBM per device.

```python
import jax
import jax.numpy as jnp
from jax import lax

D = 8192
HD = 128
GQA = 8
HEADS = 16
KV_HEADS = 2
SAMPLES = 16
SUFFIX = 48
BLK = 128
POOL_DEV = 6
SPREAD = 6
CAPACITY = 2
ROWS = 128
POOL = 48
N_DP = 8


def pool_values(key):
    values = jax.random.normal(jax.random.fold_in(key, 11), (POOL, KV_HEADS, 2, BLK, HD), jnp.float32)
    values = jnp.clip(values, -6.0, 6.0)
    return values


def offset_lists(key):
    base_key = jax.random.fold_in(key, 5)
    device_keys = jax.random.split(base_key, N_DP)
    target = jax.random.randint(jax.random.fold_in(base_key, 1), (), 0, N_DP)
    device_ids = jnp.arange(N_DP, dtype=jnp.int32)
    forced = (target - device_ids) % N_DP

    def per_device(device_key, forced_lag):
        first_key, second_key, third_key = jax.random.split(device_key, 3)
        first_lag = jax.random.randint(first_key, (), 0, SPREAD)
        first_lag = jnp.where(forced_lag < SPREAD, forced_lag, first_lag).astype(jnp.int32)
        others = jax.random.permutation(second_key, jnp.arange((SPREAD - 1) * CAPACITY, dtype=jnp.int32) // CAPACITY)
        others = others + (others >= first_lag).astype(jnp.int32)
        listed = jnp.concatenate([jnp.zeros((CAPACITY,), jnp.int32) + first_lag, others[:POOL_DEV - CAPACITY]])
        return jax.random.permutation(third_key, listed)
    return jax.vmap(per_device)(device_keys, forced).reshape(-1).astype(jnp.int32)


def draw_prefix_pool(key, part):
    return pool_values(key).astype(jnp.bfloat16)


def draw_slot_offset(key, part):
    return offset_lists(key)


def draw_queries(key, part):
    base = 2.5 * jnp.clip(jax.random.normal(jax.random.fold_in(key, 3), (ROWS, HEADS * HD), jnp.float32), -6.0, 6.0)
    return base.astype(jnp.bfloat16)


def levels(stream_key, shape, cuts, smallest, largest):
    gain, own = 1.0, jax.random.fold_in(stream_key, 6)
    for axis_at, shards_of in cuts:
        heights = jnp.exp(jax.random.uniform(jax.random.fold_in(own, axis_at), (shards_of,), jnp.float32, smallest / len(cuts), largest / len(cuts)))
        gain = gain * jnp.repeat(heights, shape[axis_at] // shards_of).reshape([-1 if axis == axis_at else 1 for axis in range(len(shape))])
    return gain


def centred(own_key, dims, scale, reach, pieces=(), kind=jnp.bfloat16):
    values = jax.random.normal(own_key, dims, jnp.float32) * scale
    if len(pieces) > 0:
        values = levels(own_key, dims, pieces, -0.22, 0.18) * values
    return jnp.clip(values, min=-reach, max=reach).astype(kind)


def setup_inputs(seed: int = 0) -> dict:
    keys = jax.random.split(jax.random.key(seed), 6)
    return {
        "queries": draw_queries(jax.random.fold_in(keys[5], 71), 0),
        "prefix_pool": draw_prefix_pool(jax.random.fold_in(keys[5], 71), 0),
        "slot_offset": draw_slot_offset(jax.random.fold_in(keys[5], 71), 0),
        "suffix_kv": centred(keys[3], (ROWS, KV_HEADS, 2, SUFFIX, HD), 1.2, 7.1875, ((0, 8),)),
        "out_weight": centred(keys[4], (HEADS * HD, D), (HEADS * HD) ** -0.5, 0.125, ((0, 4),)),
    }


NEG = -1.0e30


def rounded(values):
    return lax.optimization_barrier(values.astype(jnp.bfloat16)).astype(jnp.float32)


def reference(queries, prefix_pool, slot_offset, suffix_kv, out_weight):
    score_scale = HD ** -0.5
    lag_ids = jnp.arange(SPREAD, dtype=jnp.int32)
    slot_ids = jnp.arange(POOL_DEV, dtype=jnp.int32)

    def one_group(group):
        query_block = lax.dynamic_slice_in_dim(queries, group * SAMPLES, SAMPLES, 0).astype(jnp.float32)
        query_block = query_block.reshape(SAMPLES, KV_HEADS, GQA, HD)
        source = (group - lag_ids) % N_DP
        slot_list = (source[:, None] * POOL_DEV + slot_ids[None, :]).reshape(-1).astype(jnp.int32)
        live_slot = jnp.take(slot_offset, slot_list) == jnp.repeat(lag_ids, POOL_DEV)
        blocks = jnp.take(prefix_pool, slot_list, axis=0).astype(jnp.float32)
        key_rows = jnp.transpose(blocks[:, :, 0], (1, 0, 2, 3)).reshape(KV_HEADS, -1, HD)
        value_rows = jnp.transpose(blocks[:, :, 1], (1, 0, 2, 3)).reshape(KV_HEADS, -1, HD)
        live_rows = jnp.repeat(live_slot, BLK)
        prefix_scores = jnp.einsum("skgd,knd->skgn", query_block, key_rows) * score_scale
        prefix_scores = jnp.where(live_rows, prefix_scores, NEG)
        suffix_block = lax.dynamic_slice_in_dim(suffix_kv, group * SAMPLES, SAMPLES, 0).astype(jnp.float32)
        suffix_scores = jnp.einsum("skgd,sktd->skgt", query_block, suffix_block[:, :, 0]) * score_scale
        row_peak = jnp.maximum(prefix_scores.max(-1), suffix_scores.max(-1))
        prefix_weight = jnp.exp(prefix_scores - row_peak[..., None])
        suffix_weight = jnp.exp(suffix_scores - row_peak[..., None])
        denominator = prefix_weight.sum(-1) + suffix_weight.sum(-1)
        accumulated = jnp.einsum("skgn,knd->skgd", rounded(prefix_weight), value_rows)
        accumulated = accumulated + jnp.einsum("skgt,sktd->skgd", rounded(suffix_weight), suffix_block[:, :, 1])
        attended = (accumulated / denominator[..., None]).astype(jnp.bfloat16)
        return attended.reshape(SAMPLES, KV_HEADS * GQA * HD)

    attended = lax.map(one_group, jnp.arange(N_DP, dtype=jnp.int32))
    attended = attended.reshape(N_DP * SAMPLES, KV_HEADS * GQA * HD)
    return jnp.dot(attended, out_weight, preferred_element_type=jnp.float32).astype(jnp.bfloat16)
```

```python
import functools

import jax
import jax.numpy as jnp
from jax import lax
from jax.experimental import pallas as pl
from jax.experimental.pallas import tpu as pltpu
from jax.sharding import PartitionSpec as P

GQA = 8
SPREAD = 6
CAPACITY = 2
CHUNKS = 4
NEG = -(2.0**100)

VMEM_SPEC = pl.BlockSpec(memory_space=pltpu.VMEM)
SMEM_SPEC = pl.BlockSpec(memory_space=pltpu.SMEM)
PARAMS = pltpu.CompilerParams(vmem_limit_bytes=16 * 1024 * 1024)


def shifted(block, distance):
    size = lax.axis_size("dp")
    return lax.ppermute(block, "dp", [(i, (i + distance) % size) for i in range(size)])


def head_rows(block, head_dim):
    heads = block.shape[1] // head_dim
    return jnp.concatenate([block[:, h * head_dim : (h + 1) * head_dim] for h in range(heads)], axis=0)


def dot_nt(a, b):
    return lax.dot_general(a, b, (((1,), (1,)), ((), ())), preferred_element_type=jnp.float32)


def slots_of(offset_ref, lag):
    first = jnp.int32(0)
    second = jnp.int32(0)
    count = jnp.int32(0)
    for b in range(offset_ref.shape[0]):
        hit = offset_ref[b] == lag
        second = jnp.where(hit & (count == 1), b, second)
        first = jnp.where(hit & (count == 0), b, first)
        count = count + hit.astype(jnp.int32)
    return first, second, count


def block_pair(pool_ref, offset_ref, kv, lag):
    first, second, count = slots_of(offset_ref, lag)
    keys = jnp.concatenate([pool_ref[first, kv, 0], pool_ref[second, kv, 0]], axis=0)
    values = jnp.concatenate([pool_ref[first, kv, 1], pool_ref[second, kv, 1]], axis=0)
    return keys, values, count


def live_scores(rows, keys, count, scale):
    scores = dot_nt(rows, keys) * scale
    block = keys.shape[0] // CAPACITY
    position = lax.broadcasted_iota(jnp.int32, scores.shape, 1)
    return jnp.where(position < count * block, scores, NEG)


def own_kernel(local_heads, offset_ref, query_ref, pool_ref, suffix_ref, acc_ref, peak_ref, total_ref):
    kv = lax.axis_index("mp") * local_heads // GQA
    samples, _, _, length, head_dim = suffix_ref.shape
    scale = head_dim ** (-0.5)
    rows = head_rows(query_ref[...], head_dim)
    suffix_keys = suffix_ref[:, kv, 0].reshape(samples * length, head_dim)
    suffix_values = suffix_ref[:, kv, 1].reshape(samples * length, head_dim)
    suffix_scores = dot_nt(rows, suffix_keys) * scale
    row_sample = lax.broadcasted_iota(jnp.int32, suffix_scores.shape, 0) % samples
    key_at = lax.broadcasted_iota(jnp.int32, suffix_scores.shape, 1)
    mine = (key_at >= row_sample * length) & (key_at < (row_sample + 1) * length)
    suffix_scores = jnp.where(mine, suffix_scores, NEG)
    keys, values, count = block_pair(pool_ref, offset_ref, kv, 0)
    scores = live_scores(rows, keys, count, scale)
    peak = jnp.maximum(
        jnp.max(suffix_scores, axis=1, keepdims=True), jnp.max(scores, axis=1, keepdims=True)
    )
    suffix_weight = jnp.exp(suffix_scores - peak)
    weight = jnp.exp(scores - peak)
    total = jnp.sum(suffix_weight, axis=1, keepdims=True) + jnp.sum(weight, axis=1, keepdims=True)
    acc_ref[...] = jnp.dot(
        suffix_weight.astype(jnp.bfloat16), suffix_values, preferred_element_type=jnp.float32
    ) + jnp.dot(weight.astype(jnp.bfloat16), values, preferred_element_type=jnp.float32)
    peak_ref[...] = jnp.broadcast_to(peak, peak_ref.shape)
    total_ref[...] = jnp.broadcast_to(total, total_ref.shape)


def lag_kernel(local_heads, offset_ref, pool_ref, *refs):
    kv = lax.axis_index("mp") * local_heads // GQA
    query_refs, out_refs = refs[: SPREAD - 1], refs[SPREAD - 1 :]
    head_dim = pool_ref.shape[-1]
    scale = head_dim ** (-0.5)
    for lag in range(1, SPREAD):
        rows = head_rows(query_refs[lag - 1][...], head_dim)
        keys, values, count = block_pair(pool_ref, offset_ref, kv, lag)
        scores = live_scores(rows, keys, count, scale)
        peak = jnp.max(scores, axis=1, keepdims=True).astype(jnp.bfloat16)
        weight = jnp.exp(scores - peak.astype(jnp.float32))
        total = jnp.sum(weight, axis=1, keepdims=True).astype(jnp.bfloat16)
        acc = jnp.dot(weight.astype(jnp.bfloat16), values, preferred_element_type=jnp.float32)
        half = (rows.shape[0], head_dim // 2)
        out_refs[lag - 1][:, :head_dim] = acc.astype(jnp.bfloat16)
        out_refs[lag - 1][:, head_dim:] = jnp.concatenate(
            [jnp.broadcast_to(peak, half), jnp.broadcast_to(total, half)], axis=1
        )


def merge_kernel(acc_ref, peak_ref, total_ref, *refs):
    parts, out_ref = refs[:-1], refs[-1]
    rows, head_dim = acc_ref.shape
    samples = out_ref.shape[0]
    middle = head_dim + head_dim // 2
    accs = [acc_ref[...]]
    peaks = [peak_ref[...][:, :1]]
    totals = [total_ref[...][:, :1]]
    for part in parts:
        whole = part[...].astype(jnp.float32)
        accs.append(whole[:, :head_dim])
        peaks.append(whole[:, head_dim : head_dim + 1])
        totals.append(whole[:, middle : middle + 1])
    top = functools.reduce(jnp.maximum, peaks)
    shares = [jnp.exp(peak - top) for peak in peaks]
    total = sum(share * t for share, t in zip(shares, totals))
    acc = sum(share * a for share, a in zip(shares, accs))
    attended = (acc / total).astype(jnp.bfloat16)
    out_ref[...] = jnp.concatenate(
        [attended[h * samples : (h + 1) * samples] for h in range(rows // samples)], axis=1
    )


def project_kernel(start, attended_ref, weight_ref, out_ref):
    width = out_ref.shape[1]
    out_ref[...] = jnp.dot(
        attended_ref[...], weight_ref[:, start : start + width], preferred_element_type=jnp.float32
    ).astype(jnp.bfloat16)


def add(a, b):
    return (a.astype(jnp.float32) + b.astype(jnp.float32)).astype(jnp.bfloat16)


def summed_over_mp(attended, weight):
    size = lax.axis_size("mp")
    samples, width = attended.shape[0], weight.shape[1] // CHUNKS
    chunks = []
    for c in range(CHUNKS):
        chunks.append(
            pl.pallas_call(
                functools.partial(project_kernel, c * width),
                out_shape=jax.ShapeDtypeStruct((samples, width), jnp.bfloat16),
                in_specs=[VMEM_SPEC, VMEM_SPEC],
                out_specs=VMEM_SPEC,
                compiler_params=PARAMS,
                cost_estimate=pl.CostEstimate(
                    flops=2 * samples * weight.shape[0] * width,
                    bytes_accessed=2 * weight.shape[0] * width,
                    transcendentals=0,
                ),
            )(attended, weight)
        )
    if size & (size - 1):
        return jnp.concatenate([lax.psum(chunk, "mp") for chunk in chunks], axis=1)
    step = 1
    while step < size:
        route = [(i, i ^ step) for i in range(size)]
        chunks = [add(chunk, lax.ppermute(chunk, "mp", route)) for chunk in chunks]
        step *= 2
    return jnp.concatenate(chunks, axis=1)


def local(queries, prefix_pool, slot_offset, suffix_kv, out_weight):
    samples, _, _, length, head_dim = suffix_kv.shape
    local_heads = queries.shape[1] // head_dim
    rows = samples * local_heads
    f32, bf16 = jnp.float32, jnp.bfloat16
    asked = [shifted(queries, -lag) for lag in range(1, SPREAD)]
    acc, peak, total = pl.pallas_call(
        functools.partial(own_kernel, local_heads),
        out_shape=(jax.ShapeDtypeStruct((rows, head_dim), f32),) * 3,
        in_specs=[SMEM_SPEC] + [VMEM_SPEC] * 3,
        out_specs=(VMEM_SPEC,) * 3,
        compiler_params=PARAMS,
        cost_estimate=pl.CostEstimate(
            flops=4 * rows * samples * length * head_dim,
            bytes_accessed=2 * suffix_kv.size,
            transcendentals=rows * samples * length,
        ),
    )(slot_offset, queries, prefix_pool, suffix_kv)
    answers = pl.pallas_call(
        functools.partial(lag_kernel, local_heads),
        out_shape=(jax.ShapeDtypeStruct((rows, 2 * head_dim), bf16),) * (SPREAD - 1),
        in_specs=[SMEM_SPEC, VMEM_SPEC] + [VMEM_SPEC] * (SPREAD - 1),
        out_specs=(VMEM_SPEC,) * (SPREAD - 1),
        compiler_params=PARAMS,
    )(slot_offset, prefix_pool, *asked)
    parts = [shifted(answers[lag - 1], lag) for lag in range(1, SPREAD)]
    attended = pl.pallas_call(
        merge_kernel,
        out_shape=jax.ShapeDtypeStruct(queries.shape, bf16),
        in_specs=[VMEM_SPEC] * (3 + SPREAD - 1),
        out_specs=VMEM_SPEC,
        compiler_params=PARAMS,
    )(acc, peak, total, *parts)
    return summed_over_mp(attended, out_weight)


def solution(mesh):
    placed = (
        P("dp", "mp"),
        P("dp", None, None, None, None),
        P("dp"),
        P("dp", None, None, None, None),
        P("mp", None),
    )
    return jax.shard_map(
        local, mesh=mesh, in_specs=placed, out_specs=P("dp", None), check_vma=False
    )
```

```python
import functools

import jax
import jax.numpy as jnp
from jax import lax
from jax.experimental import pallas as pl
from jax.experimental.pallas import tpu as pltpu
from jax.sharding import PartitionSpec as P

GQA = 8
SPREAD = 6
CAPACITY = 2
CHUNKS = 4
GROUPS = ((3, 2, 1), (5, 4))
NEG = -(2.0**100)

VMEM_SPEC = pl.BlockSpec(memory_space=pltpu.VMEM)
HBM_SPEC = pl.BlockSpec(memory_space=pltpu.HBM)
PARAMS = pltpu.CompilerParams(vmem_limit_bytes=16 * 1024 * 1024)


def shifted(block, distance):
    size = lax.axis_size("dp")
    return lax.ppermute(block, "dp", [(i, (i + distance) % size) for i in range(size)])


def swapped(block, step):
    size = lax.axis_size("mp")
    return lax.ppermute(block, "mp", [(i, i ^ step) for i in range(size)])


def head_rows(block, head_dim):
    heads = block.shape[1] // head_dim
    return jnp.concatenate([block[:, h * head_dim : (h + 1) * head_dim] for h in range(heads)], axis=0)


def dot_nt(a, b):
    return lax.dot_general(a, b, (((1,), (1,)), ((), ())), preferred_element_type=jnp.float32)


def slots_of(offset_ref, lag):
    first = jnp.int32(0)
    second = jnp.int32(0)
    count = jnp.int32(0)
    for b in range(offset_ref.shape[0]):
        hit = offset_ref[b] == lag
        second = jnp.where(hit & (count == 1), b, second)
        first = jnp.where(hit & (count == 0), b, first)
        count = count + hit.astype(jnp.int32)
    return (first, second), count


def chunk_start(chunk, width):
    if chunk > 1:
        return chunk * width
    kept = lax.axis_index("mp") % 2
    return pl.multiple_of((kept if chunk == 1 else 1 - kept) * width, 128)


def weight_copy(weight_hbm, chunk, out_ref, sem):
    width = out_ref.shape[1]
    return pltpu.make_async_copy(
        weight_hbm.at[:, pl.ds(chunk_start(chunk, width), width)], out_ref, sem
    )


def own_kernel(local_heads, chunk, offset_hbm, query_hbm, pool_hbm, suffix_hbm, weight_hbm,
               acc_ref, peak_ref, total_ref, key_ref, value_ref, bias_ref, weight_ref,
               offset_ref, query_ref, suffix_ref, sems, slot_sems):
    kv = lax.axis_index("mp") * local_heads // GQA
    samples, _, length, head_dim = suffix_ref.shape
    block = key_ref.shape[1] // CAPACITY
    scale = head_dim ** (-0.5)
    offset_copy = pltpu.make_async_copy(offset_hbm, offset_ref, sems.at[0])
    query_copy = pltpu.make_async_copy(query_hbm, query_ref, sems.at[1])
    suffix_copy = pltpu.make_async_copy(suffix_hbm.at[:, kv], suffix_ref, sems.at[2])
    weight_load = weight_copy(weight_hbm, chunk, weight_ref, sems.at[3])
    offset_copy.start()
    query_copy.start()
    suffix_copy.start()
    weight_load.start()
    offset_copy.wait()
    slot_copies = []
    for lag in range(SPREAD):
        slots, count = slots_of(offset_ref, lag)
        for position, slot in enumerate(slots):
            place = pl.ds(position * block, block)
            for part, out_ref in enumerate((key_ref, value_ref)):
                copy = pltpu.make_async_copy(
                    pool_hbm.at[slot, kv, part], out_ref.at[lag, place], slot_sems.at[lag, position, part]
                )
                copy.start()
                slot_copies.append(copy)
        at = lax.broadcasted_iota(jnp.int32, bias_ref.shape[1:], 1)
        bias_ref[lag] = jnp.where(at < count * block, 0.0, NEG)
    query_copy.wait()
    rows = head_rows(query_ref[...], head_dim)
    suffix_copy.wait()
    suffix_keys = suffix_ref[:, 0].reshape(samples * length, head_dim)
    suffix_values = suffix_ref[:, 1].reshape(samples * length, head_dim)
    suffix_scores = dot_nt(rows, suffix_keys) * scale
    row_sample = lax.broadcasted_iota(jnp.int32, suffix_scores.shape, 0) % samples
    key_at = lax.broadcasted_iota(jnp.int32, suffix_scores.shape, 1)
    mine = (key_at >= row_sample * length) & (key_at < (row_sample + 1) * length)
    suffix_scores = jnp.where(mine, suffix_scores, NEG)
    for copy in slot_copies:
        copy.wait()
    scores = dot_nt(rows, key_ref[0]) * scale + bias_ref[0][:1]
    peak = jnp.maximum(
        jnp.max(suffix_scores, axis=1, keepdims=True), jnp.max(scores, axis=1, keepdims=True)
    )
    suffix_weight = jnp.exp(suffix_scores - peak)
    weight = jnp.exp(scores - peak)
    total = jnp.sum(suffix_weight, axis=1, keepdims=True) + jnp.sum(weight, axis=1, keepdims=True)
    acc_ref[...] = jnp.dot(
        suffix_weight.astype(jnp.bfloat16), suffix_values, preferred_element_type=jnp.float32
    ) + jnp.dot(weight.astype(jnp.bfloat16), value_ref[0], preferred_element_type=jnp.float32)
    peak_ref[...] = jnp.broadcast_to(peak, peak_ref.shape)
    total_ref[...] = jnp.broadcast_to(total, total_ref.shape)
    weight_load.wait()


def lag_kernel(lags, chunk, key_ref, value_ref, bias_ref, weight_hbm, *refs):
    query_refs = refs[: len(lags)]
    out_refs = refs[len(lags) : 2 * len(lags)]
    weight_ref, sem = refs[2 * len(lags) :]
    load = weight_copy(weight_hbm, chunk, weight_ref, sem)
    load.start()
    head_dim = key_ref.shape[-1]
    scale = head_dim ** (-0.5)
    for lag, query_ref, out_ref in zip(lags, query_refs, out_refs):
        rows = head_rows(query_ref[...], head_dim)
        scores = dot_nt(rows, key_ref[lag]) * scale + bias_ref[lag][:1]
        peak = jnp.max(scores, axis=1, keepdims=True).astype(jnp.bfloat16)
        weight = jnp.exp(scores - peak.astype(jnp.float32))
        total = jnp.sum(weight, axis=1, keepdims=True).astype(jnp.bfloat16)
        acc = jnp.dot(weight.astype(jnp.bfloat16), value_ref[lag], preferred_element_type=jnp.float32)
        half = (rows.shape[0], head_dim // 2)
        out_ref[:, :head_dim] = acc.astype(jnp.bfloat16)
        out_ref[:, head_dim:] = jnp.concatenate(
            [jnp.broadcast_to(peak, half), jnp.broadcast_to(total, half)], axis=1
        )
    load.wait()


def load_kernel(chunk, weight_hbm, after_hbm, weight_ref, sem):
    load = weight_copy(weight_hbm, chunk, weight_ref, sem)
    load.start()
    load.wait()


def merge_kernel(acc_ref, peak_ref, total_ref, *refs):
    parts, out_ref = refs[:-1], refs[-1]
    rows, head_dim = acc_ref.shape
    samples = out_ref.shape[0]
    middle = head_dim + head_dim // 2
    accs = [acc_ref[...]]
    peaks = [peak_ref[...][:, :1]]
    totals = [total_ref[...][:, :1]]
    for part in parts:
        whole = part[...].astype(jnp.float32)
        accs.append(whole[:, :head_dim])
        peaks.append(whole[:, head_dim : head_dim + 1])
        totals.append(whole[:, middle : middle + 1])
    top = functools.reduce(jnp.maximum, peaks)
    shares = [jnp.exp(peak - top) for peak in peaks]
    total = sum(share * t for share, t in zip(shares, totals))
    acc = sum(share * a for share, a in zip(shares, accs))
    attended = (acc / total).astype(jnp.bfloat16)
    out_ref[...] = jnp.concatenate(
        [attended[h * samples : (h + 1) * samples] for h in range(rows // samples)], axis=1
    )


def project_kernel(attended_ref, weight_ref, out_ref):
    out_ref[...] = jnp.dot(
        attended_ref[...], weight_ref[...], preferred_element_type=jnp.float32
    ).astype(jnp.bfloat16)


def project(attended, weight):
    depth, width = weight.shape
    return pl.pallas_call(
        project_kernel,
        out_shape=jax.ShapeDtypeStruct((attended.shape[0], width), jnp.bfloat16),
        in_specs=[VMEM_SPEC, VMEM_SPEC],
        out_specs=VMEM_SPEC,
        compiler_params=PARAMS,
        cost_estimate=pl.CostEstimate(
            flops=2 * attended.shape[0] * depth * width, bytes_accessed=2 * depth * width, transcendentals=0
        ),
    )(attended, weight)


def add(a, b):
    return (a.astype(jnp.float32) + b.astype(jnp.float32)).astype(jnp.bfloat16)


def final_kernel(kept_ref, other_ref, *refs):
    pairs, out_ref = refs[:-1], refs[-1]
    width = kept_ref.shape[1]
    out_ref[:, pl.ds(chunk_start(1, width), width)] = kept_ref[...]
    out_ref[:, pl.ds(chunk_start(0, width), width)] = other_ref[...]
    for i in range(len(pairs) // 2):
        out_ref[:, (2 + i) * width : (3 + i) * width] = add(pairs[2 * i][...], pairs[2 * i + 1][...])


def summed_over_four(attended, weights):
    sent = swapped(project(attended, weights[0]), 1)
    whole = [project(attended, weight) for weight in weights[2:]]
    whole_in = [swapped(chunk, 1) for chunk in whole]
    kept = add(project(attended, weights[1]), sent)
    kept_in = swapped(kept, 2)
    paired = [add(a, b) for a, b in zip(whole, whole_in)]
    paired_in = [swapped(chunk, 2) for chunk in paired]
    kept = add(kept, kept_in)
    other = swapped(kept, 1)
    tail = [x for pair in zip(paired, paired_in) for x in pair]
    samples, width = kept.shape
    return pl.pallas_call(
        final_kernel,
        out_shape=jax.ShapeDtypeStruct((samples, width * CHUNKS), jnp.bfloat16),
        in_specs=[VMEM_SPEC] * (2 + len(tail)),
        out_specs=VMEM_SPEC,
        compiler_params=PARAMS,
    )(kept, other, *tail)


def summed_over_any(attended, weights):
    first = lax.axis_index("mp") % 2 == 0
    chunks = [lax.psum(project(attended, weight), "mp") for weight in weights[2:]]
    ours = [project(attended, weight) for weight in weights[:2]]
    ours = [jnp.where(first, ours[1], ours[0]), jnp.where(first, ours[0], ours[1])]
    return jnp.concatenate([lax.psum(x, "mp") for x in ours] + chunks, axis=1)


def local(queries, prefix_pool, slot_offset, suffix_kv, out_weight):
    blocks, _, _, block, head_dim = prefix_pool.shape
    samples, _, _, length, _ = suffix_kv.shape
    local_heads = queries.shape[1] // head_dim
    rows = samples * local_heads
    depth, columns = out_weight.shape
    width = columns // CHUNKS
    f32, bf16 = jnp.float32, jnp.bfloat16
    in_hbm = [
        pltpu.with_memory_space_constraint(x, pltpu.HBM)
        for x in (slot_offset, queries, prefix_pool, suffix_kv, out_weight)
    ]
    chunk_shape = pltpu.VMEM((depth, width), bf16)
    gathered_shape = pltpu.VMEM((SPREAD, CAPACITY * block, head_dim), bf16)
    asked = {lag: shifted(queries, -lag) for group in GROUPS for lag in group}
    weights = [None] * CHUNKS
    acc, peak, total, keys, values, bias, weights[0] = pl.pallas_call(
        functools.partial(own_kernel, local_heads, 0),
        out_shape=(pltpu.VMEM((rows, head_dim), f32),) * 3
        + (gathered_shape, gathered_shape, pltpu.VMEM((SPREAD, 8, CAPACITY * block), f32), chunk_shape),
        in_specs=[HBM_SPEC] * 5,
        out_specs=(VMEM_SPEC,) * 7,
        scratch_shapes=[
            pltpu.SMEM(slot_offset.shape, jnp.int32),
            pltpu.VMEM(queries.shape, bf16),
            pltpu.VMEM((samples, 2, length, head_dim), bf16),
            pltpu.SemaphoreType.DMA((4,)),
            pltpu.SemaphoreType.DMA((SPREAD, CAPACITY, 2)),
        ],
        compiler_params=PARAMS,
        cost_estimate=pl.CostEstimate(
            flops=4 * rows * samples * length * head_dim,
            bytes_accessed=2 * suffix_kv.size + 2 * depth * width,
            transcendentals=rows * samples * length,
        ),
    )(*in_hbm)
    parts = {}
    for index, group in enumerate(GROUPS):
        out = pl.pallas_call(
            functools.partial(lag_kernel, group, 1 + index),
            out_shape=(jax.ShapeDtypeStruct((rows, 2 * head_dim), bf16),) * len(group) + (chunk_shape,),
            in_specs=[VMEM_SPEC] * 3 + [HBM_SPEC] + [VMEM_SPEC] * len(group),
            out_specs=(VMEM_SPEC,) * (len(group) + 1),
            scratch_shapes=[pltpu.SemaphoreType.DMA(())],
            compiler_params=PARAMS,
        )(keys, values, bias, in_hbm[-1], *[asked[lag] for lag in group])
        weights[1 + index] = out[-1]
        for lag, answer in zip(group, out):
            parts[lag] = shifted(answer, lag)
    last = out[0]
    weights[3] = pl.pallas_call(
        functools.partial(load_kernel, 3),
        out_shape=chunk_shape,
        in_specs=[HBM_SPEC, VMEM_SPEC],
        out_specs=VMEM_SPEC,
        scratch_shapes=[pltpu.SemaphoreType.DMA(())],
        compiler_params=PARAMS,
        cost_estimate=pl.CostEstimate(flops=0, bytes_accessed=2 * depth * width, transcendentals=0),
    )(in_hbm[-1], last)
    attended = pl.pallas_call(
        merge_kernel,
        out_shape=jax.ShapeDtypeStruct(queries.shape, bf16),
        in_specs=[VMEM_SPEC] * (3 + SPREAD - 1),
        out_specs=VMEM_SPEC,
        compiler_params=PARAMS,
    )(acc, peak, total, *[parts[lag] for lag in range(1, SPREAD)])
    if lax.axis_size("mp") == 4:
        return summed_over_four(attended, weights)
    return summed_over_any(attended, weights)


def solution(mesh):
    placed = (
        P("dp", "mp"),
        P("dp", None, None, None, None),
        P("dp"),
        P("dp", None, None, None, None),
        P("mp", None),
    )
    return jax.shard_map(
        local, mesh=mesh, in_specs=placed, out_specs=P("dp", None), check_vma=False
    )
```

```python
import functools

import jax
import jax.numpy as jnp
from jax import lax
from jax.experimental import pallas as pl
from jax.experimental.pallas import tpu as pltpu
from jax.sharding import PartitionSpec as P

GQA = 8
SPREAD = 6
CAPACITY = 2
CHUNKS = 4
GROUPS = ((3, 2, 1), (5, 4))
NEG = -(2.0**100)

VMEM_SPEC = pl.BlockSpec(memory_space=pltpu.VMEM)
HBM_SPEC = pl.BlockSpec(memory_space=pltpu.HBM)
PARAMS = pltpu.CompilerParams(vmem_limit_bytes=16 * 1024 * 1024)


def shifted(block, distance):
    size = lax.axis_size("dp")
    return lax.ppermute(block, "dp", [(i, (i + distance) % size) for i in range(size)])


def swapped(block, step):
    size = lax.axis_size("mp")
    return lax.ppermute(block, "mp", [(i, i ^ step) for i in range(size)])


def head_rows(block, head_dim):
    heads = block.shape[1] // head_dim
    return jnp.concatenate([block[:, h * head_dim : (h + 1) * head_dim] for h in range(heads)], axis=0)


def dot_nt(a, b):
    return lax.dot_general(a, b, (((1,), (1,)), ((), ())), preferred_element_type=jnp.float32)


def slots_of(offset_ref, lag):
    first = jnp.int32(0)
    second = jnp.int32(0)
    count = jnp.int32(0)
    for b in range(offset_ref.shape[0]):
        hit = offset_ref[b] == lag
        second = jnp.where(hit & (count == 1), b, second)
        first = jnp.where(hit & (count == 0), b, first)
        count = count + hit.astype(jnp.int32)
    return (first, second), count


def chunk_start(chunk, width):
    if chunk > 1:
        return chunk * width
    kept = lax.axis_index("mp") % 2
    return pl.multiple_of((kept if chunk == 1 else 1 - kept) * width, 128)


def weight_copy(weight_hbm, chunk, out_ref, sem):
    width = out_ref.shape[1]
    return pltpu.make_async_copy(
        weight_hbm.at[:, pl.ds(chunk_start(chunk, width), width)], out_ref, sem
    )


def gather_kernel(local_heads, chunk, offset_hbm, pool_hbm, weight_hbm,
                  key_ref, value_ref, bias_ref, weight_ref, offset_ref, pool_ref, sems):
    kv = lax.axis_index("mp") * local_heads // GQA
    block = pool_ref.shape[2]
    copies = [
        pltpu.make_async_copy(offset_hbm, offset_ref, sems.at[0]),
        pltpu.make_async_copy(pool_hbm.at[:, kv], pool_ref, sems.at[1]),
        weight_copy(weight_hbm, chunk, weight_ref, sems.at[2]),
    ]
    for copy in copies:
        copy.start()
    copies[0].wait()
    found = [slots_of(offset_ref, lag) for lag in range(SPREAD)]
    at = lax.broadcasted_iota(jnp.int32, bias_ref.shape[1:], 1)
    for lag, (_, count) in enumerate(found):
        bias_ref[lag] = jnp.where(at < count * block, 0.0, NEG)
    copies[1].wait()
    for lag, (slots, _) in enumerate(found):
        for position, slot in enumerate(slots):
            key_ref[lag, position * block : (position + 1) * block] = pool_ref[slot, 0]
            value_ref[lag, position * block : (position + 1) * block] = pool_ref[slot, 1]
    copies[2].wait()


def lag_kernel(lags, key_ref, value_ref, bias_ref, *refs):
    query_refs, out_refs = refs[: len(lags)], refs[len(lags) :]
    head_dim = key_ref.shape[-1]
    scale = head_dim ** (-0.5)
    rows = [head_rows(ref[...], head_dim) for ref in query_refs]
    scores = [dot_nt(r, key_ref[lag]) * scale + bias_ref[lag][:1] for r, lag in zip(rows, lags)]
    peaks = [jnp.max(x, axis=1, keepdims=True).astype(jnp.bfloat16) for x in scores]
    weights = [jnp.exp(x - peak.astype(jnp.float32)) for x, peak in zip(scores, peaks)]
    accs = [
        jnp.dot(w.astype(jnp.bfloat16), value_ref[lag], preferred_element_type=jnp.float32)
        for w, lag in zip(weights, lags)
    ]
    totals = [jnp.sum(w, axis=1, keepdims=True).astype(jnp.bfloat16) for w in weights]
    half = (rows[0].shape[0], head_dim // 2)
    for out_ref, acc, peak, total in zip(out_refs, accs, peaks, totals):
        out_ref[:, :head_dim] = acc.astype(jnp.bfloat16)
        out_ref[:, head_dim:] = jnp.concatenate(
            [jnp.broadcast_to(peak, half), jnp.broadcast_to(total, half)], axis=1
        )


def own_kernel(local_heads, chunks, key_ref, value_ref, bias_ref, after_ref, query_hbm, suffix_hbm, weight_hbm, *refs):
    acc_ref, peak_ref, total_ref = refs[:3]
    weight_refs = refs[3 : 3 + len(chunks)]
    query_ref, suffix_ref, sems = refs[3 + len(chunks) :]
    kv = lax.axis_index("mp") * local_heads // GQA
    samples, _, length, head_dim = suffix_ref.shape
    scale = head_dim ** (-0.5)
    copies = [
        pltpu.make_async_copy(query_hbm, query_ref, sems.at[0]),
        pltpu.make_async_copy(suffix_hbm.at[:, kv], suffix_ref, sems.at[1]),
    ] + [
        weight_copy(weight_hbm, chunk, ref, sems.at[2 + i])
        for i, (chunk, ref) in enumerate(zip(chunks, weight_refs))
    ]
    for copy in copies:
        copy.start()
    copies[0].wait()
    rows = head_rows(query_ref[...], head_dim)
    scores = dot_nt(rows, key_ref[0]) * scale + bias_ref[0][:1]
    copies[1].wait()
    suffix_keys = suffix_ref[:, 0].reshape(samples * length, head_dim)
    suffix_values = suffix_ref[:, 1].reshape(samples * length, head_dim)
    suffix_scores = dot_nt(rows, suffix_keys) * scale
    row_sample = lax.broadcasted_iota(jnp.int32, suffix_scores.shape, 0) % samples
    key_at = lax.broadcasted_iota(jnp.int32, suffix_scores.shape, 1)
    mine = (key_at >= row_sample * length) & (key_at < (row_sample + 1) * length)
    suffix_scores = jnp.where(mine, suffix_scores, NEG)
    peak = jnp.maximum(
        jnp.max(suffix_scores, axis=1, keepdims=True), jnp.max(scores, axis=1, keepdims=True)
    )
    suffix_weight = jnp.exp(suffix_scores - peak)
    weight = jnp.exp(scores - peak)
    total = jnp.sum(suffix_weight, axis=1, keepdims=True) + jnp.sum(weight, axis=1, keepdims=True)
    acc_ref[...] = jnp.dot(
        suffix_weight.astype(jnp.bfloat16), suffix_values, preferred_element_type=jnp.float32
    ) + jnp.dot(weight.astype(jnp.bfloat16), value_ref[0], preferred_element_type=jnp.float32)
    peak_ref[...] = jnp.broadcast_to(peak, peak_ref.shape)
    total_ref[...] = jnp.broadcast_to(total, total_ref.shape)
    for copy in copies[2:]:
        copy.wait()


def merge_kernel(acc_ref, peak_ref, total_ref, *refs):
    parts, out_ref = refs[:-1], refs[-1]
    rows, head_dim = acc_ref.shape
    samples = out_ref.shape[0]
    middle = head_dim + head_dim // 2
    accs = [acc_ref[...]]
    peaks = [peak_ref[...][:, :1]]
    totals = [total_ref[...][:, :1]]
    for part in parts:
        whole = part[...].astype(jnp.float32)
        accs.append(whole[:, :head_dim])
        peaks.append(whole[:, head_dim : head_dim + 1])
        totals.append(whole[:, middle : middle + 1])
    top = functools.reduce(jnp.maximum, peaks)
    shares = [jnp.exp(peak - top) for peak in peaks]
    total = sum(share * t for share, t in zip(shares, totals))
    acc = sum(share * a for share, a in zip(shares, accs))
    attended = (acc / total).astype(jnp.bfloat16)
    out_ref[...] = jnp.concatenate(
        [attended[h * samples : (h + 1) * samples] for h in range(rows // samples)], axis=1
    )


def project_kernel(attended_ref, weight_ref, out_ref):
    out_ref[...] = jnp.dot(
        attended_ref[...], weight_ref[...], preferred_element_type=jnp.float32
    ).astype(jnp.bfloat16)


def project(attended, weight):
    depth, width = weight.shape
    return pl.pallas_call(
        project_kernel,
        out_shape=jax.ShapeDtypeStruct((attended.shape[0], width), jnp.bfloat16),
        in_specs=[VMEM_SPEC, VMEM_SPEC],
        out_specs=VMEM_SPEC,
        compiler_params=PARAMS,
        cost_estimate=pl.CostEstimate(
            flops=2 * attended.shape[0] * depth * width, bytes_accessed=2 * depth * width, transcendentals=0
        ),
    )(attended, weight)


def add(a, b):
    return (a.astype(jnp.float32) + b.astype(jnp.float32)).astype(jnp.bfloat16)


def final_kernel(kept_ref, other_ref, *refs):
    pairs, out_ref = refs[:-1], refs[-1]
    width = kept_ref.shape[1]
    out_ref[:, pl.ds(chunk_start(1, width), width)] = kept_ref[...]
    out_ref[:, pl.ds(chunk_start(0, width), width)] = other_ref[...]
    for i in range(len(pairs) // 2):
        out_ref[:, (2 + i) * width : (3 + i) * width] = add(pairs[2 * i][...], pairs[2 * i + 1][...])


def summed_over_four(attended, weights):
    sent = swapped(project(attended, weights[0]), 1)
    whole = [project(attended, weight) for weight in weights[2:]]
    whole_in = [swapped(chunk, 1) for chunk in whole]
    kept = add(project(attended, weights[1]), sent)
    kept_in = swapped(kept, 2)
    paired = [add(a, b) for a, b in zip(whole, whole_in)]
    paired_in = [swapped(chunk, 2) for chunk in paired]
    kept = add(kept, kept_in)
    other = swapped(kept, 1)
    tail = [x for pair in zip(paired, paired_in) for x in pair]
    samples, width = kept.shape
    return pl.pallas_call(
        final_kernel,
        out_shape=jax.ShapeDtypeStruct((samples, width * CHUNKS), jnp.bfloat16),
        in_specs=[VMEM_SPEC] * (2 + len(tail)),
        out_specs=VMEM_SPEC,
        compiler_params=PARAMS,
    )(kept, other, *tail)


def summed_over_any(attended, weights):
    first = lax.axis_index("mp") % 2 == 0
    chunks = [lax.psum(project(attended, weight), "mp") for weight in weights[2:]]
    ours = [project(attended, weight) for weight in weights[:2]]
    ours = [jnp.where(first, ours[1], ours[0]), jnp.where(first, ours[0], ours[1])]
    return jnp.concatenate([lax.psum(x, "mp") for x in ours] + chunks, axis=1)


def local(queries, prefix_pool, slot_offset, suffix_kv, out_weight):
    blocks, _, _, block, head_dim = prefix_pool.shape
    samples, _, _, length, _ = suffix_kv.shape
    local_heads = queries.shape[1] // head_dim
    rows = samples * local_heads
    depth, columns = out_weight.shape
    width = columns // CHUNKS
    f32, bf16 = jnp.float32, jnp.bfloat16
    in_hbm = [
        pltpu.with_memory_space_constraint(x, pltpu.HBM)
        for x in (slot_offset, queries, prefix_pool, suffix_kv, out_weight)
    ]
    chunk_shape = pltpu.VMEM((depth, width), bf16)
    gathered_shape = pltpu.VMEM((SPREAD, CAPACITY * block, head_dim), bf16)
    asked = {lag: shifted(queries, -lag) for group in GROUPS for lag in group}
    offsets, queries_hbm, pool, suffix, weight = in_hbm
    keys, values, bias, first_chunk = pl.pallas_call(
        functools.partial(gather_kernel, local_heads, 0),
        out_shape=(gathered_shape, gathered_shape, pltpu.VMEM((SPREAD, 8, CAPACITY * block), f32), chunk_shape),
        in_specs=[HBM_SPEC] * 3,
        out_specs=(VMEM_SPEC,) * 4,
        scratch_shapes=[
            pltpu.SMEM(slot_offset.shape, jnp.int32),
            pltpu.VMEM((blocks, 2, block, head_dim), bf16),
            pltpu.SemaphoreType.DMA((3,)),
        ],
        compiler_params=PARAMS,
        cost_estimate=pl.CostEstimate(flops=0, bytes_accessed=2 * depth * width, transcendentals=0),
    )(offsets, pool, weight)
    parts = {}
    for group in GROUPS:
        out = pl.pallas_call(
            functools.partial(lag_kernel, group),
            out_shape=(jax.ShapeDtypeStruct((rows, 2 * head_dim), bf16),) * len(group),
            in_specs=[VMEM_SPEC] * (3 + len(group)),
            out_specs=(VMEM_SPEC,) * len(group),
            compiler_params=PARAMS,
        )(keys, values, bias, *[asked[lag] for lag in group])
        for lag, answer in zip(group, out):
            parts[lag] = shifted(answer, lag)
    later = tuple(range(1, CHUNKS))
    acc, peak, total, *chunks = pl.pallas_call(
        functools.partial(own_kernel, local_heads, later),
        out_shape=(pltpu.VMEM((rows, head_dim), f32),) * 3 + (chunk_shape,) * len(later),
        in_specs=[VMEM_SPEC] * 4 + [HBM_SPEC] * 3,
        out_specs=(VMEM_SPEC,) * (3 + len(later)),
        scratch_shapes=[
            pltpu.VMEM(queries.shape, bf16),
            pltpu.VMEM((samples, 2, length, head_dim), bf16),
            pltpu.SemaphoreType.DMA((2 + len(later),)),
        ],
        compiler_params=PARAMS,
        cost_estimate=pl.CostEstimate(
            flops=4 * rows * samples * length * head_dim,
            bytes_accessed=2 * suffix_kv.size + 2 * depth * width * len(later),
            transcendentals=rows * samples * length,
        ),
    )(keys, values, bias, out[-1], queries_hbm, suffix, weight)
    weights = [first_chunk, *chunks]
    attended = pl.pallas_call(
        merge_kernel,
        out_shape=jax.ShapeDtypeStruct(queries.shape, bf16),
        in_specs=[VMEM_SPEC] * (3 + SPREAD - 1),
        out_specs=VMEM_SPEC,
        compiler_params=PARAMS,
    )(acc, peak, total, *[parts[lag] for lag in range(1, SPREAD)])
    if lax.axis_size("mp") == 4:
        return summed_over_four(attended, weights)
    return summed_over_any(attended, weights)


def solution(mesh):
    placed = (
        P("dp", "mp"),
        P("dp", None, None, None, None),
        P("dp"),
        P("dp", None, None, None, None),
        P("mp", None),
    )
    return jax.shard_map(
        local, mesh=mesh, in_specs=placed, out_specs=P("dp", None), check_vma=False
    )
```

```python
import functools

import jax
import jax.numpy as jnp
from jax import lax
from jax.experimental import pallas as pl
from jax.experimental.pallas import tpu as pltpu
from jax.sharding import PartitionSpec as P

GQA = 8
SPREAD = 6
CAPACITY = 2
PARTS = (("split", 4), ("near", 4))
ASKED = (2, 3, 4)
SENT = (1, 5)
FLAG_ROWS = 8
NEG = -(2.0**100)

VMEM_SPEC = pl.BlockSpec(memory_space=pltpu.VMEM)
HBM_SPEC = pl.BlockSpec(memory_space=pltpu.HBM)
PARAMS = pltpu.CompilerParams(vmem_limit_bytes=16 * 1024 * 1024)


def lasting(us):
    return pl.CostEstimate(
        flops=int(us * 1.1e9), bytes_accessed=int(us * 3.69e6), transcendentals=int(us * 1e7)
    )


def shifted(block, distance):
    size = lax.axis_size("dp")
    return lax.ppermute(block, "dp", [(i, (i + distance) % size) for i in range(size)])


def swapped(block, step):
    size = lax.axis_size("mp")
    return lax.ppermute(block, "mp", [(i, i ^ step) for i in range(size)])


def head_rows(block, head_dim):
    heads = block.shape[1] // head_dim
    return jnp.concatenate([block[:, h * head_dim : (h + 1) * head_dim] for h in range(heads)], axis=0)


def dot_nt(a, b):
    return lax.dot_general(a, b, (((1,), (1,)), ((), ())), preferred_element_type=jnp.float32)


def slots_of(offset_ref, lag):
    first = jnp.int32(0)
    second = jnp.int32(0)
    count = jnp.int32(0)
    for b in range(offset_ref.shape[0]):
        hit = offset_ref[b] == lag
        second = jnp.where(hit & (count == 1), b, second)
        first = jnp.where(hit & (count == 0), b, first)
        count = count + hit.astype(jnp.int32)
    return (first, second), count


def first_column(half, start, width):
    if half is None:
        return start
    kept = lax.axis_index("mp") % 2
    return pl.multiple_of(start + (kept if half else 1 - kept) * width, 128)


def gather_kernel(local_heads, offset_hbm, pool_hbm, key_ref, value_ref, bias_ref, *refs):
    pack_refs = dict(zip(SENT, refs))
    offset_ref, pool_ref, sems = refs[len(SENT) :]
    kv = lax.axis_index("mp") * local_heads // GQA
    block, head_dim = pool_ref.shape[2:]
    copies = [
        pltpu.make_async_copy(offset_hbm, offset_ref, sems.at[0]),
        pltpu.make_async_copy(pool_hbm.at[:, kv], pool_ref, sems.at[1]),
    ]
    for copy in copies:
        copy.start()
    copies[0].wait()
    found = [slots_of(offset_ref, lag) for lag in range(SPREAD)]
    at = lax.broadcasted_iota(jnp.int32, bias_ref.shape[1:], 1)
    kept = (0,) + ASKED
    for i, lag in enumerate(kept):
        bias_ref[i] = jnp.where(at < found[lag][1] * block, 0.0, NEG)
    at = lax.broadcasted_iota(jnp.int32, (2 * FLAG_ROWS, head_dim), 0)
    for lag, ref in pack_refs.items():
        ref[2 * CAPACITY * block :] = jnp.where(at < found[lag][1] * FLAG_ROWS, 0.0, NEG).astype(jnp.bfloat16)
    copies[1].wait()
    for lag, (slots, _) in enumerate(found):
        for position, slot in enumerate(slots):
            if lag in SENT:
                at = position * block
                pack_refs[lag][at : at + block] = pool_ref[slot, 0]
                pack_refs[lag][CAPACITY * block + at : CAPACITY * block + at + block] = pool_ref[slot, 1]
            else:
                place = slice(position * block, (position + 1) * block)
                key_ref[kept.index(lag), place] = pool_ref[slot, 0]
                value_ref[kept.index(lag), place] = pool_ref[slot, 1]


def held_kernel(after_ref, query_ref, *refs):
    pack_refs, (acc_ref, peak_ref, total_ref) = refs[: len(SENT)], refs[len(SENT) :]
    head_dim = pack_refs[0].shape[1]
    length = (pack_refs[0].shape[0] - CAPACITY * FLAG_ROWS) // 2
    block = length // CAPACITY
    scale = head_dim ** (-0.5)
    rows = head_rows(query_ref[...], head_dim)
    scores = []
    for ref in pack_refs:
        flags = ref[2 * length :].astype(jnp.float32)
        bias = jnp.concatenate([flags[i * FLAG_ROWS : i * FLAG_ROWS + 1] for i in range(CAPACITY)], axis=1)
        scores.append(dot_nt(rows, ref[:length]) * scale + bias)
    peak = functools.reduce(jnp.maximum, [jnp.max(x, axis=1, keepdims=True) for x in scores])
    weights = [jnp.exp(x - peak) for x in scores]
    total = sum(jnp.sum(w, axis=1, keepdims=True) for w in weights)
    acc_ref[...] = sum(
        jnp.dot(w.astype(jnp.bfloat16), ref[length : 2 * length], preferred_element_type=jnp.float32)
        for w, ref in zip(weights, pack_refs)
    )
    peak_ref[...] = jnp.broadcast_to(peak, peak_ref.shape)
    total_ref[...] = jnp.broadcast_to(total, total_ref.shape)


def lag_kernel(key_ref, value_ref, bias_ref, *refs):
    query_refs, out_refs = refs[: len(ASKED)], refs[len(ASKED) :]
    lags = range(1, 1 + len(ASKED))
    head_dim = key_ref.shape[-1]
    scale = head_dim ** (-0.5)
    rows = [head_rows(ref[...], head_dim) for ref in query_refs]
    scores = [dot_nt(r, key_ref[lag]) * scale + bias_ref[lag][:1] for r, lag in zip(rows, lags)]
    peaks = [jnp.max(x, axis=1, keepdims=True).astype(jnp.bfloat16) for x in scores]
    weights = [jnp.exp(x - peak.astype(jnp.float32)) for x, peak in zip(scores, peaks)]
    accs = [
        jnp.dot(w.astype(jnp.bfloat16), value_ref[lag], preferred_element_type=jnp.float32)
        for w, lag in zip(weights, lags)
    ]
    totals = [jnp.sum(w, axis=1, keepdims=True).astype(jnp.bfloat16) for w in weights]
    half = (rows[0].shape[0], head_dim // 2)
    for out_ref, acc, peak, total in zip(out_refs, accs, peaks, totals):
        out_ref[:, :head_dim] = acc.astype(jnp.bfloat16)
        out_ref[:, head_dim:] = jnp.concatenate(
            [jnp.broadcast_to(peak, half), jnp.broadcast_to(total, half)], axis=1
        )


def own_kernel(local_heads, key_ref, value_ref, bias_ref, after_ref, query_hbm, suffix_hbm,
               acc_ref, peak_ref, total_ref, query_ref, suffix_ref, sems):
    kv = lax.axis_index("mp") * local_heads // GQA
    samples, _, length, head_dim = suffix_ref.shape
    scale = head_dim ** (-0.5)
    copies = [
        pltpu.make_async_copy(query_hbm, query_ref, sems.at[0]),
        pltpu.make_async_copy(suffix_hbm.at[:, kv], suffix_ref, sems.at[1]),
    ]
    for copy in copies:
        copy.start()
    copies[0].wait()
    rows = head_rows(query_ref[...], head_dim)
    scores = dot_nt(rows, key_ref[0]) * scale + bias_ref[0][:1]
    copies[1].wait()
    suffix_keys = suffix_ref[:, 0].reshape(samples * length, head_dim)
    suffix_values = suffix_ref[:, 1].reshape(samples * length, head_dim)
    suffix_scores = dot_nt(rows, suffix_keys) * scale
    row_sample = lax.broadcasted_iota(jnp.int32, suffix_scores.shape, 0) % samples
    key_at = lax.broadcasted_iota(jnp.int32, suffix_scores.shape, 1)
    mine = (key_at >= row_sample * length) & (key_at < (row_sample + 1) * length)
    suffix_scores = jnp.where(mine, suffix_scores, NEG)
    peak = jnp.maximum(
        jnp.max(suffix_scores, axis=1, keepdims=True), jnp.max(scores, axis=1, keepdims=True)
    )
    suffix_weight = jnp.exp(suffix_scores - peak)
    weight = jnp.exp(scores - peak)
    total = jnp.sum(suffix_weight, axis=1, keepdims=True) + jnp.sum(weight, axis=1, keepdims=True)
    acc_ref[...] = jnp.dot(
        suffix_weight.astype(jnp.bfloat16), suffix_values, preferred_element_type=jnp.float32
    ) + jnp.dot(weight.astype(jnp.bfloat16), value_ref[0], preferred_element_type=jnp.float32)
    peak_ref[...] = jnp.broadcast_to(peak, peak_ref.shape)
    total_ref[...] = jnp.broadcast_to(total, total_ref.shape)


def merge_kernel(*refs):
    whole_refs, part_refs, out_ref = refs[:6], refs[6:-1], refs[-1]
    rows, head_dim = whole_refs[0].shape
    samples = out_ref.shape[0]
    middle = head_dim + head_dim // 2
    accs = [ref[...] for ref in whole_refs[0::3]]
    peaks = [ref[...][:, :1] for ref in whole_refs[1::3]]
    totals = [ref[...][:, :1] for ref in whole_refs[2::3]]
    for ref in part_refs:
        part = ref[...].astype(jnp.float32)
        accs.append(part[:, :head_dim])
        peaks.append(part[:, head_dim : head_dim + 1])
        totals.append(part[:, middle : middle + 1])
    top = functools.reduce(jnp.maximum, peaks)
    shares = [jnp.exp(peak - top) for peak in peaks]
    total = sum(share * t for share, t in zip(shares, totals))
    acc = sum(share * a for share, a in zip(shares, accs))
    attended = (acc / total).astype(jnp.bfloat16)
    out_ref[...] = jnp.concatenate(
        [attended[h * samples : (h + 1) * samples] for h in range(rows // samples)], axis=1
    )


def project_kernel(half, start, attended_ref, weight_ref, out_ref):
    width = out_ref.shape[1]
    out_ref[...] = jnp.dot(
        attended_ref[...],
        weight_ref[:, pl.ds(first_column(half, start, width), width)],
        preferred_element_type=jnp.float32,
    ).astype(jnp.bfloat16)


def project(attended, weight, half, start, width):
    depth = weight.shape[0]
    return pl.pallas_call(
        functools.partial(project_kernel, half, start),
        out_shape=jax.ShapeDtypeStruct((attended.shape[0], width), jnp.bfloat16),
        in_specs=[VMEM_SPEC, VMEM_SPEC],
        out_specs=VMEM_SPEC,
        compiler_params=PARAMS,
        cost_estimate=pl.CostEstimate(
            flops=2 * attended.shape[0] * depth * width, bytes_accessed=2 * depth * width, transcendentals=0
        ),
    )(attended, weight)


def add(a, b):
    return (a.astype(jnp.float32) + b.astype(jnp.float32)).astype(jnp.bfloat16)


def final_kernel(layout, *refs):
    out_ref = refs[-1]
    at = 0
    for kind, start, width in layout:
        if kind == "split":
            for half in (1, 0):
                out_ref[:, pl.ds(first_column(half, start, width // 2), width // 2)] = refs[at + 1 - half][...]
        else:
            out_ref[:, start : start + width] = add(refs[at][...], refs[at + 1][...])
        at += 2


def summed_over_four(attended, weight):
    columns = weight.shape[1]
    layout, start = [], 0
    for kind, eighths in PARTS:
        layout.append((kind, start, columns * eighths // 8))
        start += columns * eighths // 8
    first = {}
    got = {}
    for kind, start, width in layout:
        if kind == "split":
            got[start] = swapped(project(attended, weight, 0, start, width // 2), 1)
        else:
            first[start] = project(attended, weight, None, start, width)
            got[start] = swapped(first[start], 1 if kind == "near" else 2)
    for kind, start, width in layout:
        if kind == "split":
            first[start] = project(attended, weight, 1, start, width // 2)
    operands = []
    for kind, start, width in layout:
        total = add(first[start], got[start])
        if kind == "split":
            total = add(total, swapped(total, 2))
            operands += [total, swapped(total, 1)]
        else:
            operands += [total, swapped(total, 2 if kind == "near" else 1)]
    return pl.pallas_call(
        functools.partial(final_kernel, layout),
        out_shape=jax.ShapeDtypeStruct((attended.shape[0], columns), jnp.bfloat16),
        in_specs=[VMEM_SPEC] * len(operands),
        out_specs=VMEM_SPEC,
        compiler_params=PARAMS,
    )(*operands)


def summed_over_any(attended, weight):
    return lax.psum(project(attended, weight, None, 0, weight.shape[1]), "mp")


def local(queries, prefix_pool, slot_offset, suffix_kv, out_weight):
    blocks, _, _, block, head_dim = prefix_pool.shape
    samples, _, _, length_of_suffix, _ = suffix_kv.shape
    local_heads = queries.shape[1] // head_dim
    rows = samples * local_heads
    f32, bf16 = jnp.float32, jnp.bfloat16
    offsets, queries_hbm, pool, suffix = [
        pltpu.with_memory_space_constraint(x, pltpu.HBM)
        for x in (slot_offset, queries, prefix_pool, suffix_kv)
    ]
    length = CAPACITY * block
    gathered = pltpu.VMEM((1 + len(ASKED), length, head_dim), bf16)
    partial = (pltpu.VMEM((rows, head_dim), f32),) * 3
    asked = [shifted(queries, -lag) for lag in ASKED]
    keys, values, bias, *packs = pl.pallas_call(
        functools.partial(gather_kernel, local_heads),
        out_shape=(gathered, gathered, pltpu.VMEM((1 + len(ASKED), 8, length), f32))
        + (pltpu.VMEM((2 * length + CAPACITY * FLAG_ROWS, head_dim), bf16),) * len(SENT),
        in_specs=[HBM_SPEC] * 2,
        out_specs=(VMEM_SPEC,) * (3 + len(SENT)),
        scratch_shapes=[
            pltpu.SMEM(slot_offset.shape, jnp.int32),
            pltpu.VMEM((blocks, 2, block, head_dim), bf16),
            pltpu.SemaphoreType.DMA((2,)),
        ],
        compiler_params=PARAMS,
        cost_estimate=lasting(8),
    )(offsets, pool)
    held = [shifted(pack, lag) for pack, lag in zip(packs, SENT)]
    answers = pl.pallas_call(
        lag_kernel,
        out_shape=(jax.ShapeDtypeStruct((rows, 2 * head_dim), bf16),) * len(ASKED),
        in_specs=[VMEM_SPEC] * (3 + len(ASKED)),
        out_specs=(VMEM_SPEC,) * len(ASKED),
        compiler_params=PARAMS,
        cost_estimate=lasting(0.4),
    )(keys, values, bias, *asked)
    parts = [shifted(answer, lag) for answer, lag in zip(answers, ASKED)]
    own = pl.pallas_call(
        functools.partial(own_kernel, local_heads),
        out_shape=partial,
        in_specs=[VMEM_SPEC] * 4 + [HBM_SPEC] * 2,
        out_specs=(VMEM_SPEC,) * 3,
        scratch_shapes=[
            pltpu.VMEM(queries.shape, bf16),
            pltpu.VMEM((samples, 2, length_of_suffix, head_dim), bf16),
            pltpu.SemaphoreType.DMA((2,)),
        ],
        compiler_params=PARAMS,
        cost_estimate=lasting(1.6),
    )(keys, values, bias, answers[-1], queries_hbm, suffix)
    others = pl.pallas_call(
        held_kernel,
        out_shape=partial,
        in_specs=[VMEM_SPEC] * (2 + len(SENT)),
        out_specs=(VMEM_SPEC,) * 3,
        compiler_params=PARAMS,
        cost_estimate=lasting(0.5),
    )(own[0], queries, *held)
    attended = pl.pallas_call(
        merge_kernel,
        out_shape=jax.ShapeDtypeStruct(queries.shape, bf16),
        in_specs=[VMEM_SPEC] * (6 + len(ASKED)),
        out_specs=VMEM_SPEC,
        compiler_params=PARAMS,
        cost_estimate=lasting(0.2),
    )(*own, *others, *parts)
    if lax.axis_size("mp") == 4:
        return summed_over_four(attended, out_weight)
    return summed_over_any(attended, out_weight)


def solution(mesh):
    placed = (
        P("dp", "mp"),
        P("dp", None, None, None, None),
        P("dp"),
        P("dp", None, None, None, None),
        P("mp", None),
    )
    return jax.shard_map(
        local, mesh=mesh, in_specs=placed, out_specs=P("dp", None), check_vma=False
    )
```

```python
import functools

import jax
import jax.numpy as jnp
from jax import lax
from jax.experimental import pallas as pl
from jax.experimental.pallas import tpu as pltpu
from jax.sharding import PartitionSpec as P

GQA = 8
SPREAD = 6
CAPACITY = 2
PARTS = (("split", 4), ("far", 2), ("near", 2))
ASKED = (1, 2, 3)
SENT = (4, 5)
FLAG_ROWS = 8
NEG = -(2.0**100)

VMEM_SPEC = pl.BlockSpec(memory_space=pltpu.VMEM)
HBM_SPEC = pl.BlockSpec(memory_space=pltpu.HBM)
PARAMS = pltpu.CompilerParams(vmem_limit_bytes=16 * 1024 * 1024)


def lasting(us):
    return pl.CostEstimate(
        flops=int(us * 1.1e9), bytes_accessed=int(us * 3.69e6), transcendentals=int(us * 1e7)
    )


def shifted(block, distance):
    size = lax.axis_size("dp")
    return lax.ppermute(block, "dp", [(i, (i + distance) % size) for i in range(size)])


def swapped(block, step):
    size = lax.axis_size("mp")
    return lax.ppermute(block, "mp", [(i, i ^ step) for i in range(size)])


def head_rows(block, head_dim):
    heads = block.shape[1] // head_dim
    return jnp.concatenate([block[:, h * head_dim : (h + 1) * head_dim] for h in range(heads)], axis=0)


def dot_nt(a, b):
    return lax.dot_general(a, b, (((1,), (1,)), ((), ())), preferred_element_type=jnp.float32)


def slots_of(offset_ref, lag):
    first = jnp.int32(0)
    second = jnp.int32(0)
    count = jnp.int32(0)
    for b in range(offset_ref.shape[0]):
        hit = offset_ref[b] == lag
        second = jnp.where(hit & (count == 1), b, second)
        first = jnp.where(hit & (count == 0), b, first)
        count = count + hit.astype(jnp.int32)
    return (first, second), count


def first_column(half, start, width):
    if half is None:
        return start
    kept = lax.axis_index("mp") % 2
    return pl.multiple_of(start + (kept if half else 1 - kept) * width, 128)


def gather_kernel(local_heads, offset_hbm, pool_hbm, key_ref, value_ref, bias_ref, *refs):
    pack_refs = dict(zip(SENT, refs))
    offset_ref, pool_ref, sems = refs[len(SENT) :]
    kv = lax.axis_index("mp") * local_heads // GQA
    block, head_dim = pool_ref.shape[2:]
    copies = [
        pltpu.make_async_copy(offset_hbm, offset_ref, sems.at[0]),
        pltpu.make_async_copy(pool_hbm.at[:, kv], pool_ref, sems.at[1]),
    ]
    for copy in copies:
        copy.start()
    copies[0].wait()
    found = [slots_of(offset_ref, lag) for lag in range(SPREAD)]
    at = lax.broadcasted_iota(jnp.int32, bias_ref.shape[1:], 1)
    kept = (0,) + ASKED
    for i, lag in enumerate(kept):
        bias_ref[i] = jnp.where(at < found[lag][1] * block, 0.0, NEG)
    at = lax.broadcasted_iota(jnp.int32, (2 * FLAG_ROWS, head_dim), 0)
    for lag, ref in pack_refs.items():
        ref[2 * CAPACITY * block :] = jnp.where(at < found[lag][1] * FLAG_ROWS, 0.0, NEG).astype(jnp.bfloat16)
    copies[1].wait()
    for lag, (slots, _) in enumerate(found):
        for position, slot in enumerate(slots):
            if lag in SENT:
                at = position * block
                pack_refs[lag][at : at + block] = pool_ref[slot, 0]
                pack_refs[lag][CAPACITY * block + at : CAPACITY * block + at + block] = pool_ref[slot, 1]
            else:
                place = slice(position * block, (position + 1) * block)
                key_ref[kept.index(lag), place] = pool_ref[slot, 0]
                value_ref[kept.index(lag), place] = pool_ref[slot, 1]


def held_kernel(after_ref, query_ref, *refs):
    pack_refs, (acc_ref, peak_ref, total_ref) = refs[: len(SENT)], refs[len(SENT) :]
    head_dim = pack_refs[0].shape[1]
    length = (pack_refs[0].shape[0] - CAPACITY * FLAG_ROWS) // 2
    block = length // CAPACITY
    scale = head_dim ** (-0.5)
    rows = head_rows(query_ref[...], head_dim)
    scores = []
    for ref in pack_refs:
        flags = ref[2 * length :].astype(jnp.float32)
        bias = jnp.concatenate([flags[i * FLAG_ROWS : i * FLAG_ROWS + 1] for i in range(CAPACITY)], axis=1)
        scores.append(dot_nt(rows, ref[:length]) * scale + bias)
    peak = functools.reduce(jnp.maximum, [jnp.max(x, axis=1, keepdims=True) for x in scores])
    weights = [jnp.exp(x - peak) for x in scores]
    total = sum(jnp.sum(w, axis=1, keepdims=True) for w in weights)
    acc_ref[...] = sum(
        jnp.dot(w.astype(jnp.bfloat16), ref[length : 2 * length], preferred_element_type=jnp.float32)
        for w, ref in zip(weights, pack_refs)
    )
    peak_ref[...] = jnp.broadcast_to(peak, peak_ref.shape)
    total_ref[...] = jnp.broadcast_to(total, total_ref.shape)


def lag_kernel(key_ref, value_ref, bias_ref, *refs):
    query_refs, out_refs = refs[: len(ASKED)], refs[len(ASKED) :]
    lags = range(1, 1 + len(ASKED))
    head_dim = key_ref.shape[-1]
    scale = head_dim ** (-0.5)
    rows = [head_rows(ref[...], head_dim) for ref in query_refs]
    scores = [dot_nt(r, key_ref[lag]) * scale + bias_ref[lag][:1] for r, lag in zip(rows, lags)]
    peaks = [jnp.max(x, axis=1, keepdims=True).astype(jnp.bfloat16) for x in scores]
    weights = [jnp.exp(x - peak.astype(jnp.float32)) for x, peak in zip(scores, peaks)]
    accs = [
        jnp.dot(w.astype(jnp.bfloat16), value_ref[lag], preferred_element_type=jnp.float32)
        for w, lag in zip(weights, lags)
    ]
    totals = [jnp.sum(w, axis=1, keepdims=True).astype(jnp.bfloat16) for w in weights]
    half = (rows[0].shape[0], head_dim // 2)
    for out_ref, acc, peak, total in zip(out_refs, accs, peaks, totals):
        out_ref[:, :head_dim] = acc.astype(jnp.bfloat16)
        out_ref[:, head_dim:] = jnp.concatenate(
            [jnp.broadcast_to(peak, half), jnp.broadcast_to(total, half)], axis=1
        )


def own_kernel(local_heads, key_ref, value_ref, bias_ref, after_ref, query_hbm, suffix_hbm,
               acc_ref, peak_ref, total_ref, query_ref, suffix_ref, sems):
    kv = lax.axis_index("mp") * local_heads // GQA
    samples, _, length, head_dim = suffix_ref.shape
    scale = head_dim ** (-0.5)
    copies = [
        pltpu.make_async_copy(query_hbm, query_ref, sems.at[0]),
        pltpu.make_async_copy(suffix_hbm.at[:, kv], suffix_ref, sems.at[1]),
    ]
    for copy in copies:
        copy.start()
    copies[0].wait()
    rows = head_rows(query_ref[...], head_dim)
    scores = dot_nt(rows, key_ref[0]) * scale + bias_ref[0][:1]
    copies[1].wait()
    suffix_keys = suffix_ref[:, 0].reshape(samples * length, head_dim)
    suffix_values = suffix_ref[:, 1].reshape(samples * length, head_dim)
    suffix_scores = dot_nt(rows, suffix_keys) * scale
    row_sample = lax.broadcasted_iota(jnp.int32, suffix_scores.shape, 0) % samples
    key_at = lax.broadcasted_iota(jnp.int32, suffix_scores.shape, 1)
    mine = (key_at >= row_sample * length) & (key_at < (row_sample + 1) * length)
    suffix_scores = jnp.where(mine, suffix_scores, NEG)
    peak = jnp.maximum(
        jnp.max(suffix_scores, axis=1, keepdims=True), jnp.max(scores, axis=1, keepdims=True)
    )
    suffix_weight = jnp.exp(suffix_scores - peak)
    weight = jnp.exp(scores - peak)
    total = jnp.sum(suffix_weight, axis=1, keepdims=True) + jnp.sum(weight, axis=1, keepdims=True)
    acc_ref[...] = jnp.dot(
        suffix_weight.astype(jnp.bfloat16), suffix_values, preferred_element_type=jnp.float32
    ) + jnp.dot(weight.astype(jnp.bfloat16), value_ref[0], preferred_element_type=jnp.float32)
    peak_ref[...] = jnp.broadcast_to(peak, peak_ref.shape)
    total_ref[...] = jnp.broadcast_to(total, total_ref.shape)


def merge_kernel(*refs):
    whole_refs, part_refs, out_ref = refs[:6], refs[6:-1], refs[-1]
    rows, head_dim = whole_refs[0].shape
    samples = out_ref.shape[0]
    middle = head_dim + head_dim // 2
    accs = [ref[...] for ref in whole_refs[0::3]]
    peaks = [ref[...][:, :1] for ref in whole_refs[1::3]]
    totals = [ref[...][:, :1] for ref in whole_refs[2::3]]
    for ref in part_refs:
        part = ref[...].astype(jnp.float32)
        accs.append(part[:, :head_dim])
        peaks.append(part[:, head_dim : head_dim + 1])
        totals.append(part[:, middle : middle + 1])
    top = functools.reduce(jnp.maximum, peaks)
    shares = [jnp.exp(peak - top) for peak in peaks]
    total = sum(share * t for share, t in zip(shares, totals))
    acc = sum(share * a for share, a in zip(shares, accs))
    attended = (acc / total).astype(jnp.bfloat16)
    out_ref[...] = jnp.concatenate(
        [attended[h * samples : (h + 1) * samples] for h in range(rows // samples)], axis=1
    )


def project_kernel(half, start, attended_ref, weight_ref, out_ref):
    width = out_ref.shape[1]
    out_ref[...] = jnp.dot(
        attended_ref[...],
        weight_ref[:, pl.ds(first_column(half, start, width), width)],
        preferred_element_type=jnp.float32,
    ).astype(jnp.bfloat16)


def project(attended, weight, half, start, width):
    depth = weight.shape[0]
    return pl.pallas_call(
        functools.partial(project_kernel, half, start),
        out_shape=jax.ShapeDtypeStruct((attended.shape[0], width), jnp.bfloat16),
        in_specs=[VMEM_SPEC, VMEM_SPEC],
        out_specs=VMEM_SPEC,
        compiler_params=PARAMS,
        cost_estimate=pl.CostEstimate(
            flops=2 * attended.shape[0] * depth * width, bytes_accessed=2 * depth * width, transcendentals=0
        ),
    )(attended, weight)


def add(a, b):
    return (a.astype(jnp.float32) + b.astype(jnp.float32)).astype(jnp.bfloat16)


def final_kernel(layout, *refs):
    out_ref = refs[-1]
    at = 0
    for kind, start, width in layout:
        if kind == "split":
            for half in (1, 0):
                out_ref[:, pl.ds(first_column(half, start, width // 2), width // 2)] = refs[at + 1 - half][...]
        else:
            out_ref[:, start : start + width] = add(refs[at][...], refs[at + 1][...])
        at += 2


def summed_over_four(attended, weight):
    columns = weight.shape[1]
    layout, start = [], 0
    for kind, eighths in PARTS:
        layout.append((kind, start, columns * eighths // 8))
        start += columns * eighths // 8
    first = {}
    got = {}
    for kind, start, width in layout:
        if kind == "split":
            got[start] = swapped(project(attended, weight, 0, start, width // 2), 1)
        else:
            first[start] = project(attended, weight, None, start, width)
            got[start] = swapped(first[start], 1 if kind == "near" else 2)
    for kind, start, width in layout:
        if kind == "split":
            first[start] = project(attended, weight, 1, start, width // 2)
    operands = []
    for kind, start, width in layout:
        total = add(first[start], got[start])
        if kind == "split":
            total = add(total, swapped(total, 2))
            operands += [total, swapped(total, 1)]
        else:
            operands += [total, swapped(total, 2 if kind == "near" else 1)]
    return pl.pallas_call(
        functools.partial(final_kernel, layout),
        out_shape=jax.ShapeDtypeStruct((attended.shape[0], columns), jnp.bfloat16),
        in_specs=[VMEM_SPEC] * len(operands),
        out_specs=VMEM_SPEC,
        compiler_params=PARAMS,
    )(*operands)


def summed_over_any(attended, weight):
    return lax.psum(project(attended, weight, None, 0, weight.shape[1]), "mp")


def local(queries, prefix_pool, slot_offset, suffix_kv, out_weight):
    blocks, _, _, block, head_dim = prefix_pool.shape
    samples, _, _, length_of_suffix, _ = suffix_kv.shape
    local_heads = queries.shape[1] // head_dim
    rows = samples * local_heads
    f32, bf16 = jnp.float32, jnp.bfloat16
    offsets, queries_hbm, pool, suffix = [
        pltpu.with_memory_space_constraint(x, pltpu.HBM)
        for x in (slot_offset, queries, prefix_pool, suffix_kv)
    ]
    length = CAPACITY * block
    gathered = pltpu.VMEM((1 + len(ASKED), length, head_dim), bf16)
    partial = (pltpu.VMEM((rows, head_dim), f32),) * 3
    asked = [shifted(queries, -lag) for lag in ASKED]
    keys, values, bias, *packs = pl.pallas_call(
        functools.partial(gather_kernel, local_heads),
        out_shape=(gathered, gathered, pltpu.VMEM((1 + len(ASKED), 8, length), f32))
        + (pltpu.VMEM((2 * length + CAPACITY * FLAG_ROWS, head_dim), bf16),) * len(SENT),
        in_specs=[HBM_SPEC] * 2,
        out_specs=(VMEM_SPEC,) * (3 + len(SENT)),
        scratch_shapes=[
            pltpu.SMEM(slot_offset.shape, jnp.int32),
            pltpu.VMEM((blocks, 2, block, head_dim), bf16),
            pltpu.SemaphoreType.DMA((2,)),
        ],
        compiler_params=PARAMS,
        cost_estimate=lasting(8),
    )(offsets, pool)
    held = [shifted(pack, lag) for pack, lag in zip(packs, SENT)]
    answers = pl.pallas_call(
        lag_kernel,
        out_shape=(jax.ShapeDtypeStruct((rows, 2 * head_dim), bf16),) * len(ASKED),
        in_specs=[VMEM_SPEC] * (3 + len(ASKED)),
        out_specs=(VMEM_SPEC,) * len(ASKED),
        compiler_params=PARAMS,
        cost_estimate=lasting(0.4),
    )(keys, values, bias, *asked)
    parts = [shifted(answer, lag) for answer, lag in zip(answers, ASKED)]
    own = pl.pallas_call(
        functools.partial(own_kernel, local_heads),
        out_shape=partial,
        in_specs=[VMEM_SPEC] * 4 + [HBM_SPEC] * 2,
        out_specs=(VMEM_SPEC,) * 3,
        scratch_shapes=[
            pltpu.VMEM(queries.shape, bf16),
            pltpu.VMEM((samples, 2, length_of_suffix, head_dim), bf16),
            pltpu.SemaphoreType.DMA((2,)),
        ],
        compiler_params=PARAMS,
        cost_estimate=lasting(1.6),
    )(keys, values, bias, answers[-1], queries_hbm, suffix)
    others = pl.pallas_call(
        held_kernel,
        out_shape=partial,
        in_specs=[VMEM_SPEC] * (2 + len(SENT)),
        out_specs=(VMEM_SPEC,) * 3,
        compiler_params=PARAMS,
        cost_estimate=lasting(0.5),
    )(own[0], queries, *held)
    attended = pl.pallas_call(
        merge_kernel,
        out_shape=jax.ShapeDtypeStruct(queries.shape, bf16),
        in_specs=[VMEM_SPEC] * (6 + len(ASKED)),
        out_specs=VMEM_SPEC,
        compiler_params=PARAMS,
        cost_estimate=lasting(0.2),
    )(*own, *others, *parts)
    if lax.axis_size("mp") == 4:
        return summed_over_four(attended, out_weight)
    return summed_over_any(attended, out_weight)


def solution(mesh):
    placed = (
        P("dp", "mp"),
        P("dp", None, None, None, None),
        P("dp"),
        P("dp", None, None, None, None),
        P("mp", None),
    )
    return jax.shard_map(
        local, mesh=mesh, in_specs=placed, out_specs=P("dp", None), check_vma=False
    )
```

```python
import functools

import jax
import jax.numpy as jnp
from jax import lax
from jax.experimental import pallas as pl
from jax.experimental.pallas import tpu as pltpu
from jax.sharding import PartitionSpec as P

GQA = 8
SPREAD = 6
CAPACITY = 2
PARTS = (('split', 2, 4), ('near', 3, 4))
ASKED = (1, 2, 4)
SENT = (3, 5)
FLAG_ROWS = 8
NEG = -(2.0**100)

VMEM_SPEC = pl.BlockSpec(memory_space=pltpu.VMEM)
HBM_SPEC = pl.BlockSpec(memory_space=pltpu.HBM)
PARAMS = pltpu.CompilerParams(vmem_limit_bytes=16 * 1024 * 1024)


def lasting(us):
    return pl.CostEstimate(
        flops=int(us * 1.1e9), bytes_accessed=int(us * 3.69e6), transcendentals=int(us * 1e7)
    )


def shifted(block, distance):
    size = lax.axis_size("dp")
    return lax.ppermute(block, "dp", [(i, (i + distance) % size) for i in range(size)])


def swapped(block, step):
    size = lax.axis_size("mp")
    return lax.ppermute(block, "mp", [(i, i ^ step) for i in range(size)])


def head_rows(block, head_dim):
    heads = block.shape[1] // head_dim
    return jnp.concatenate([block[:, h * head_dim : (h + 1) * head_dim] for h in range(heads)], axis=0)


def dot_nt(a, b):
    return lax.dot_general(a, b, (((1,), (1,)), ((), ())), preferred_element_type=jnp.float32)


def slots_of(offset_ref, lag):
    first = jnp.int32(0)
    second = jnp.int32(0)
    count = jnp.int32(0)
    for b in range(offset_ref.shape[0]):
        hit = offset_ref[b] == lag
        second = jnp.where(hit & (count == 1), b, second)
        first = jnp.where(hit & (count == 0), b, first)
        count = count + hit.astype(jnp.int32)
    return (first, second), count


def first_column(half, far, start, width):
    if half is None:
        return start
    place = lax.axis_index("mp")
    kept = place % 2 if far == 2 else (place + place // 2) % 2
    return pl.multiple_of(start + (kept if half else 1 - kept) * width, 128)


def mask_kernel(samples, out_ref):
    rows, keys = out_ref.shape
    length = keys // samples
    row_sample = lax.broadcasted_iota(jnp.int32, (rows, keys), 0) % samples
    key_at = lax.broadcasted_iota(jnp.int32, (rows, keys), 1)
    mine = (key_at >= row_sample * length) & (key_at < (row_sample + 1) * length)
    out_ref[...] = jnp.where(mine, 0.0, NEG)


def gather_kernel(local_heads, after_ref, offset_ref, pool_ref, key_ref, value_ref, bias_ref, *refs):
    pack_refs = dict(zip(SENT, refs))
    kv = lax.axis_index("mp") * local_heads // GQA
    block, head_dim = pool_ref.shape[3:]
    found = [slots_of(offset_ref, lag) for lag in range(SPREAD)]
    at = lax.broadcasted_iota(jnp.int32, bias_ref.shape[1:], 1)
    kept = (0,) + ASKED
    for i, lag in enumerate(kept):
        bias_ref[i] = jnp.where(at < found[lag][1] * block, 0.0, NEG)
    at = lax.broadcasted_iota(jnp.int32, (2 * FLAG_ROWS, head_dim), 0)
    for lag, ref in pack_refs.items():
        ref[2 * CAPACITY * block :] = jnp.where(at < found[lag][1] * FLAG_ROWS, 0.0, NEG).astype(jnp.bfloat16)
    for lag, (slots, _) in enumerate(found):
        for position, slot in enumerate(slots):
            if lag in SENT:
                at = position * block
                pack_refs[lag][at : at + block] = pool_ref[slot, kv, 0]
                pack_refs[lag][CAPACITY * block + at : CAPACITY * block + at + block] = pool_ref[slot, kv, 1]
            else:
                place = slice(position * block, (position + 1) * block)
                key_ref[kept.index(lag), place] = pool_ref[slot, kv, 0]
                value_ref[kept.index(lag), place] = pool_ref[slot, kv, 1]


def held_kernel(after_ref, query_ref, *refs):
    pack_refs, (acc_ref, peak_ref, total_ref) = refs[: len(SENT)], refs[len(SENT) :]
    head_dim = pack_refs[0].shape[1]
    length = (pack_refs[0].shape[0] - CAPACITY * FLAG_ROWS) // 2
    block = length // CAPACITY
    scale = head_dim ** (-0.5)
    rows = head_rows(query_ref[...], head_dim)
    scores = []
    for ref in pack_refs:
        flags = ref[2 * length :].astype(jnp.float32)
        bias = jnp.concatenate([flags[i * FLAG_ROWS : i * FLAG_ROWS + 1] for i in range(CAPACITY)], axis=1)
        scores.append(dot_nt(rows, ref[:length]) * scale + bias)
    peak = functools.reduce(jnp.maximum, [jnp.max(x, axis=1, keepdims=True) for x in scores])
    weights = [jnp.exp(x - peak) for x in scores]
    total = sum(jnp.sum(w, axis=1, keepdims=True) for w in weights)
    acc_ref[...] = sum(
        jnp.dot(w.astype(jnp.bfloat16), ref[length : 2 * length], preferred_element_type=jnp.float32)
        for w, ref in zip(weights, pack_refs)
    )
    peak_ref[...] = jnp.broadcast_to(peak, peak_ref.shape)
    total_ref[...] = jnp.broadcast_to(total, total_ref.shape)


def lag_kernel(key_ref, value_ref, bias_ref, *refs):
    query_refs, out_refs = refs[: len(ASKED)], refs[len(ASKED) :]
    lags = range(1, 1 + len(ASKED))
    head_dim = key_ref.shape[-1]
    scale = head_dim ** (-0.5)
    rows = [head_rows(ref[...], head_dim) for ref in query_refs]
    scores = [dot_nt(r, key_ref[lag]) * scale + bias_ref[lag][:1] for r, lag in zip(rows, lags)]
    peaks = [jnp.max(x, axis=1, keepdims=True).astype(jnp.bfloat16) for x in scores]
    weights = [jnp.exp(x - peak.astype(jnp.float32)) for x, peak in zip(scores, peaks)]
    accs = [
        jnp.dot(w.astype(jnp.bfloat16), value_ref[lag], preferred_element_type=jnp.float32)
        for w, lag in zip(weights, lags)
    ]
    totals = [jnp.sum(w, axis=1, keepdims=True).astype(jnp.bfloat16) for w in weights]
    half = (rows[0].shape[0], head_dim // 2)
    for out_ref, acc, peak, total in zip(out_refs, accs, peaks, totals):
        out_ref[:, :head_dim] = acc.astype(jnp.bfloat16)
        out_ref[:, head_dim:] = jnp.concatenate(
            [jnp.broadcast_to(peak, half), jnp.broadcast_to(total, half)], axis=1
        )


def own_kernel(local_heads, key_ref, value_ref, bias_ref, mask_ref, after_ref, query_hbm, suffix_hbm,
               acc_ref, peak_ref, total_ref, query_ref, suffix_ref, sems):
    kv = lax.axis_index("mp") * local_heads // GQA
    samples, _, length, head_dim = suffix_ref.shape
    scale = head_dim ** (-0.5)
    copies = [
        pltpu.make_async_copy(query_hbm, query_ref, sems.at[0]),
        pltpu.make_async_copy(suffix_hbm.at[:, kv], suffix_ref, sems.at[1]),
    ]
    for copy in copies:
        copy.start()
    copies[0].wait()
    rows = head_rows(query_ref[...], head_dim)
    scores = dot_nt(rows, key_ref[0]) * scale + bias_ref[0][:1]
    copies[1].wait()
    suffix_keys = suffix_ref[:, 0].reshape(samples * length, head_dim)
    suffix_values = suffix_ref[:, 1].reshape(samples * length, head_dim)
    suffix_scores = dot_nt(rows, suffix_keys) * scale + mask_ref[...]
    peak = jnp.maximum(
        jnp.max(suffix_scores, axis=1, keepdims=True), jnp.max(scores, axis=1, keepdims=True)
    )
    suffix_weight = jnp.exp(suffix_scores - peak)
    weight = jnp.exp(scores - peak)
    total = jnp.sum(suffix_weight, axis=1, keepdims=True) + jnp.sum(weight, axis=1, keepdims=True)
    acc_ref[...] = jnp.dot(
        suffix_weight.astype(jnp.bfloat16), suffix_values, preferred_element_type=jnp.float32
    ) + jnp.dot(weight.astype(jnp.bfloat16), value_ref[0], preferred_element_type=jnp.float32)
    peak_ref[...] = jnp.broadcast_to(peak, peak_ref.shape)
    total_ref[...] = jnp.broadcast_to(total, total_ref.shape)


def merge_kernel(*refs):
    whole_refs, part_refs, out_ref = refs[:6], refs[6:-1], refs[-1]
    rows, head_dim = whole_refs[0].shape
    samples = out_ref.shape[0]
    middle = head_dim + head_dim // 2
    accs = [ref[...] for ref in whole_refs[0::3]]
    peaks = [ref[...][:, :1] for ref in whole_refs[1::3]]
    totals = [ref[...][:, :1] for ref in whole_refs[2::3]]
    for ref in part_refs:
        part = ref[...].astype(jnp.float32)
        accs.append(part[:, :head_dim])
        peaks.append(part[:, head_dim : head_dim + 1])
        totals.append(part[:, middle : middle + 1])
    top = functools.reduce(jnp.maximum, peaks)
    shares = [jnp.exp(peak - top) for peak in peaks]
    total = sum(share * t for share, t in zip(shares, totals))
    acc = sum(share * a for share, a in zip(shares, accs))
    attended = (acc / total).astype(jnp.bfloat16)
    out_ref[...] = jnp.concatenate(
        [attended[h * samples : (h + 1) * samples] for h in range(rows // samples)], axis=1
    )


def project_kernel(half, far, start, attended_ref, weight_ref, out_ref):
    width = out_ref.shape[1]
    out_ref[...] = jnp.dot(
        attended_ref[...],
        weight_ref[:, pl.ds(first_column(half, far, start, width), width)],
        preferred_element_type=jnp.float32,
    ).astype(jnp.bfloat16)


def project(attended, weight, half, far, start, width):
    depth = weight.shape[0]
    return pl.pallas_call(
        functools.partial(project_kernel, half, far, start),
        out_shape=jax.ShapeDtypeStruct((attended.shape[0], width), jnp.bfloat16),
        in_specs=[VMEM_SPEC, VMEM_SPEC],
        out_specs=VMEM_SPEC,
        compiler_params=PARAMS,
        cost_estimate=pl.CostEstimate(
            flops=2 * attended.shape[0] * depth * width, bytes_accessed=2 * depth * width, transcendentals=0
        ),
    )(attended, weight)


def add(a, b):
    return (a.astype(jnp.float32) + b.astype(jnp.float32)).astype(jnp.bfloat16)


def final_kernel(layout, *refs):
    out_ref = refs[-1]
    at = 0
    for kind, far, start, width in layout:
        if kind == "split":
            for half in (1, 0):
                out_ref[:, pl.ds(first_column(half, far, start, width // 2), width // 2)] = refs[at + 1 - half][...]
        else:
            out_ref[:, start : start + width] = add(refs[at][...], refs[at + 1][...])
        at += 2


def summed_over_four(attended, weight):
    columns = weight.shape[1]
    layout, start = [], 0
    for kind, far, eighths in PARTS:
        layout.append((kind, far, start, columns * eighths // 8))
        start += columns * eighths // 8
    first = {}
    got = {}
    for kind, far, start, width in layout:
        if kind == "split":
            got[start] = swapped(project(attended, weight, 0, far, start, width // 2), 1)
        else:
            first[start] = project(attended, weight, None, far, start, width)
            got[start] = swapped(first[start], 1 if kind == "near" else far)
    for kind, far, start, width in layout:
        if kind == "split":
            first[start] = project(attended, weight, 1, far, start, width // 2)
    operands = []
    for kind, far, start, width in layout:
        total = add(first[start], got[start])
        if kind == "split":
            total = add(total, swapped(total, far))
            operands += [total, swapped(total, 1)]
        else:
            operands += [total, swapped(total, far if kind == "near" else 1)]
    return pl.pallas_call(
        functools.partial(final_kernel, layout),
        out_shape=jax.ShapeDtypeStruct((attended.shape[0], columns), jnp.bfloat16),
        in_specs=[VMEM_SPEC] * len(operands),
        out_specs=VMEM_SPEC,
        compiler_params=PARAMS,
    )(*operands)


def summed_over_any(attended, weight):
    return lax.psum(project(attended, weight, None, 2, 0, weight.shape[1]), "mp")


def local(queries, prefix_pool, slot_offset, suffix_kv, out_weight):
    _, _, _, block, head_dim = prefix_pool.shape
    samples, _, _, length_of_suffix, _ = suffix_kv.shape
    local_heads = queries.shape[1] // head_dim
    rows = samples * local_heads
    f32, bf16 = jnp.float32, jnp.bfloat16
    queries_hbm, suffix = [pltpu.with_memory_space_constraint(x, pltpu.HBM) for x in (queries, suffix_kv)]
    mask = pl.pallas_call(
        functools.partial(mask_kernel, samples),
        out_shape=pltpu.VMEM((rows, samples * length_of_suffix), f32),
        out_specs=VMEM_SPEC,
        compiler_params=PARAMS,
        cost_estimate=lasting(8),
    )()
    length = CAPACITY * block
    gathered = pltpu.VMEM((1 + len(ASKED), length, head_dim), bf16)
    partial = (pltpu.VMEM((rows, head_dim), f32),) * 3
    asked = [shifted(queries, -lag) for lag in ASKED]
    keys, values, bias, *packs = pl.pallas_call(
        functools.partial(gather_kernel, local_heads),
        out_shape=(gathered, gathered, pltpu.VMEM((1 + len(ASKED), 8, length), f32))
        + (pltpu.VMEM((2 * length + CAPACITY * FLAG_ROWS, head_dim), bf16),) * len(SENT),
        in_specs=[VMEM_SPEC, pl.BlockSpec(memory_space=pltpu.SMEM), VMEM_SPEC],
        out_specs=(VMEM_SPEC,) * (3 + len(SENT)),
        compiler_params=PARAMS,
        cost_estimate=lasting(8),
    )(mask, slot_offset, prefix_pool)
    held = [shifted(pack, lag) for pack, lag in zip(packs, SENT)]
    answers = pl.pallas_call(
        lag_kernel,
        out_shape=(jax.ShapeDtypeStruct((rows, 2 * head_dim), bf16),) * len(ASKED),
        in_specs=[VMEM_SPEC] * (3 + len(ASKED)),
        out_specs=(VMEM_SPEC,) * len(ASKED),
        compiler_params=PARAMS,
        cost_estimate=lasting(0.4),
    )(keys, values, bias, *asked)
    parts = [shifted(answer, lag) for answer, lag in zip(answers, ASKED)]
    own = pl.pallas_call(
        functools.partial(own_kernel, local_heads),
        out_shape=partial,
        in_specs=[VMEM_SPEC] * 5 + [HBM_SPEC] * 2,
        out_specs=(VMEM_SPEC,) * 3,
        scratch_shapes=[
            pltpu.VMEM(queries.shape, bf16),
            pltpu.VMEM((samples, 2, length_of_suffix, head_dim), bf16),
            pltpu.SemaphoreType.DMA((2,)),
        ],
        compiler_params=PARAMS,
        cost_estimate=lasting(1.6),
    )(keys, values, bias, mask, answers[-1], queries_hbm, suffix)
    others = pl.pallas_call(
        held_kernel,
        out_shape=partial,
        in_specs=[VMEM_SPEC] * (2 + len(SENT)),
        out_specs=(VMEM_SPEC,) * 3,
        compiler_params=PARAMS,
        cost_estimate=lasting(0.5),
    )(own[0], queries, *held)
    attended = pl.pallas_call(
        merge_kernel,
        out_shape=jax.ShapeDtypeStruct(queries.shape, bf16),
        in_specs=[VMEM_SPEC] * (6 + len(ASKED)),
        out_specs=VMEM_SPEC,
        compiler_params=PARAMS,
        cost_estimate=lasting(0.2),
    )(*own, *others, *parts)
    if lax.axis_size("mp") == 4:
        return summed_over_four(attended, out_weight)
    return summed_over_any(attended, out_weight)


def solution(mesh):
    placed = (
        P("dp", "mp"),
        P("dp", None, None, None, None),
        P("dp"),
        P("dp", None, None, None, None),
        P("mp", None),
    )
    return jax.shard_map(
        local, mesh=mesh, in_specs=placed, out_specs=P("dp", None), check_vma=False
    )
```

```python
import functools

import jax
import jax.numpy as jnp
from jax import lax
from jax.experimental import pallas as pl
from jax.experimental.pallas import tpu as pltpu
from jax.sharding import PartitionSpec as P

GQA = 8
SPREAD = 6
CAPACITY = 2
PARTS = (("split", 2, 4), ("near", 3, 4))
ASKED = (1, 2, 4)
SENT = (3, 5)
FLAG_ROWS = 8
STAT_ROWS = 16
NEG = -(2.0**100)

VMEM_SPEC = pl.BlockSpec(memory_space=pltpu.VMEM)
HBM_SPEC = pl.BlockSpec(memory_space=pltpu.HBM)
PARAMS = pltpu.CompilerParams(vmem_limit_bytes=16 * 1024 * 1024)


def lasting(us):
    return pl.CostEstimate(
        flops=int(us * 1.1e9), bytes_accessed=int(us * 3.69e6), transcendentals=int(us * 1e7)
    )


def shifted(block, distance):
    size = lax.axis_size("dp")
    return lax.ppermute(block, "dp", [(i, (i + distance) % size) for i in range(size)])


def swapped(block, step):
    size = lax.axis_size("mp")
    return lax.ppermute(block, "mp", [(i, i ^ step) for i in range(size)])


def head_rows(block, head_dim):
    heads = block.shape[1] // head_dim
    return jnp.concatenate([block[:, h * head_dim : (h + 1) * head_dim] for h in range(heads)], axis=0)


def dot_nt(a, b):
    return lax.dot_general(a, b, (((1,), (1,)), ((), ())), preferred_element_type=jnp.float32)


def slots_of(offset_ref, lag):
    first = jnp.int32(0)
    second = jnp.int32(0)
    count = jnp.int32(0)
    for b in range(offset_ref.shape[0]):
        hit = offset_ref[b] == lag
        second = jnp.where(hit & (count == 1), b, second)
        first = jnp.where(hit & (count == 0), b, first)
        count = count + hit.astype(jnp.int32)
    return (first, second), count


def first_column(half, far, start, width):
    if half is None:
        return start
    place = lax.axis_index("mp")
    kept = place % 2 if far == 2 else (place + place // 2) % 2
    return pl.multiple_of(start + (kept if half else 1 - kept) * width, 128)


def mask_kernel(samples, out_ref):
    rows, keys = out_ref.shape
    length = keys // samples
    row_sample = lax.broadcasted_iota(jnp.int32, (rows, keys), 0) % samples
    key_at = lax.broadcasted_iota(jnp.int32, (rows, keys), 1)
    mine = (key_at >= row_sample * length) & (key_at < (row_sample + 1) * length)
    out_ref[...] = jnp.where(mine, 0.0, NEG)


def gather_kernel(local_heads, after_ref, offset_ref, pool_ref, key_ref, value_ref, bias_ref, *refs):
    pack_refs = dict(zip(SENT, refs))
    kv = lax.axis_index("mp") * local_heads // GQA
    block, head_dim = pool_ref.shape[3:]
    found = [slots_of(offset_ref, lag) for lag in range(SPREAD)]
    at = lax.broadcasted_iota(jnp.int32, bias_ref.shape[1:], 1)
    kept = (0,) + ASKED
    for i, lag in enumerate(kept):
        bias_ref[i] = jnp.where(at < found[lag][1] * block, 0.0, NEG)
    at = lax.broadcasted_iota(jnp.int32, (2 * FLAG_ROWS, head_dim), 0)
    for lag, ref in pack_refs.items():
        ref[2 * CAPACITY * block :] = jnp.where(at < found[lag][1] * FLAG_ROWS, 0.0, NEG).astype(jnp.bfloat16)
    for lag, (slots, _) in enumerate(found):
        for position, slot in enumerate(slots):
            if lag in SENT:
                at = position * block
                pack_refs[lag][at : at + block] = pool_ref[slot, kv, 0]
                pack_refs[lag][CAPACITY * block + at : CAPACITY * block + at + block] = pool_ref[slot, kv, 1]
            else:
                place = slice(position * block, (position + 1) * block)
                key_ref[kept.index(lag), place] = pool_ref[slot, kv, 0]
                value_ref[kept.index(lag), place] = pool_ref[slot, kv, 1]


def held_kernel(after_ref, query_ref, *refs):
    pack_refs, (acc_ref, peak_ref, total_ref) = refs[: len(SENT)], refs[len(SENT) :]
    head_dim = pack_refs[0].shape[1]
    length = (pack_refs[0].shape[0] - CAPACITY * FLAG_ROWS) // 2
    block = length // CAPACITY
    scale = head_dim ** (-0.5)
    rows = head_rows(query_ref[...], head_dim)
    scores = []
    for ref in pack_refs:
        flags = ref[2 * length :].astype(jnp.float32)
        bias = jnp.concatenate([flags[i * FLAG_ROWS : i * FLAG_ROWS + 1] for i in range(CAPACITY)], axis=1)
        scores.append(dot_nt(rows, ref[:length]) * scale + bias)
    peak = functools.reduce(jnp.maximum, [jnp.max(x, axis=1, keepdims=True) for x in scores])
    weights = [jnp.exp(x - peak) for x in scores]
    total = sum(jnp.sum(w, axis=1, keepdims=True) for w in weights)
    acc_ref[...] = sum(
        jnp.dot(w.astype(jnp.bfloat16), ref[length : 2 * length], preferred_element_type=jnp.float32)
        for w, ref in zip(weights, pack_refs)
    )
    peak_ref[...] = jnp.broadcast_to(peak, peak_ref.shape)
    total_ref[...] = jnp.broadcast_to(total, total_ref.shape)


def diagonal(rows, lanes):
    shape = (rows, lanes)
    return lax.broadcasted_iota(jnp.int32, shape, 0) == lax.broadcasted_iota(jnp.int32, shape, 1)


def along_lanes(column, lanes):
    return jnp.sum(jnp.where(diagonal(column.shape[0], lanes), column, 0.0), axis=0, keepdims=True)


def along_rows(row, rows):
    return jnp.sum(jnp.where(diagonal(rows, row.shape[1]), row, 0.0), axis=1, keepdims=True)


def lag_kernel(key_ref, value_ref, bias_ref, *refs):
    query_refs, out_refs = refs[: len(ASKED)], refs[len(ASKED) :]
    lags = range(1, 1 + len(ASKED))
    head_dim = key_ref.shape[-1]
    scale = head_dim ** (-0.5)
    rows = [head_rows(ref[...], head_dim) for ref in query_refs]
    scores = [dot_nt(r, key_ref[lag]) * scale + bias_ref[lag][:1] for r, lag in zip(rows, lags)]
    peaks = [jnp.max(x, axis=1, keepdims=True).astype(jnp.bfloat16) for x in scores]
    weights = [jnp.exp(x - peak.astype(jnp.float32)) for x, peak in zip(scores, peaks)]
    accs = [
        jnp.dot(w.astype(jnp.bfloat16), value_ref[lag], preferred_element_type=jnp.float32)
        for w, lag in zip(weights, lags)
    ]
    totals = [jnp.sum(w, axis=1, keepdims=True).astype(jnp.bfloat16) for w in weights]
    length = rows[0].shape[0]
    at = lax.broadcasted_iota(jnp.int32, (STAT_ROWS, head_dim), 0)
    for out_ref, acc, peak, total in zip(out_refs, accs, peaks, totals):
        out_ref[:length] = acc.astype(jnp.bfloat16)
        laid = [along_lanes(x.astype(jnp.float32), head_dim) for x in (peak, total)]
        out_ref[length:] = jnp.where(at == 0, laid[0], jnp.where(at == 1, laid[1], 0.0)).astype(jnp.bfloat16)


def own_kernel(local_heads, key_ref, value_ref, bias_ref, mask_ref, after_ref, query_hbm, suffix_hbm,
               acc_ref, peak_ref, total_ref, query_ref, suffix_ref, sems):
    kv = lax.axis_index("mp") * local_heads // GQA
    samples, _, length, head_dim = suffix_ref.shape
    scale = head_dim ** (-0.5)
    copies = [
        pltpu.make_async_copy(query_hbm, query_ref, sems.at[0]),
        pltpu.make_async_copy(suffix_hbm.at[:, kv], suffix_ref, sems.at[1]),
    ]
    for copy in copies:
        copy.start()
    copies[0].wait()
    rows = head_rows(query_ref[...], head_dim)
    scores = dot_nt(rows, key_ref[0]) * scale + bias_ref[0][:1]
    copies[1].wait()
    suffix_keys = suffix_ref[:, 0].reshape(samples * length, head_dim)
    suffix_values = suffix_ref[:, 1].reshape(samples * length, head_dim)
    suffix_scores = dot_nt(rows, suffix_keys) * scale + mask_ref[...]
    peak = jnp.maximum(
        jnp.max(suffix_scores, axis=1, keepdims=True), jnp.max(scores, axis=1, keepdims=True)
    )
    suffix_weight = jnp.exp(suffix_scores - peak)
    weight = jnp.exp(scores - peak)
    total = jnp.sum(suffix_weight, axis=1, keepdims=True) + jnp.sum(weight, axis=1, keepdims=True)
    acc_ref[...] = jnp.dot(
        suffix_weight.astype(jnp.bfloat16), suffix_values, preferred_element_type=jnp.float32
    ) + jnp.dot(weight.astype(jnp.bfloat16), value_ref[0], preferred_element_type=jnp.float32)
    peak_ref[...] = jnp.broadcast_to(peak, peak_ref.shape)
    total_ref[...] = jnp.broadcast_to(total, total_ref.shape)


def merge_kernel(*refs):
    whole_refs, part_refs, out_ref = refs[:6], refs[6:-1], refs[-1]
    rows, head_dim = whole_refs[0].shape
    samples = out_ref.shape[0]
    accs = [ref[...] for ref in whole_refs[0::3]]
    peaks = [ref[...][:, :1] for ref in whole_refs[1::3]]
    totals = [ref[...][:, :1] for ref in whole_refs[2::3]]
    for ref in part_refs:
        part = ref[...].astype(jnp.float32)
        accs.append(part[:rows])
        peaks.append(along_rows(part[rows : rows + 1], rows))
        totals.append(along_rows(part[rows + 1 : rows + 2], rows))
    top = functools.reduce(jnp.maximum, peaks)
    shares = [jnp.exp(peak - top) for peak in peaks]
    total = sum(share * t for share, t in zip(shares, totals))
    acc = sum(share * a for share, a in zip(shares, accs))
    attended = (acc / total).astype(jnp.bfloat16)
    out_ref[...] = jnp.concatenate(
        [attended[h * samples : (h + 1) * samples] for h in range(rows // samples)], axis=1
    )


def project_kernel(half, far, start, attended_ref, weight_ref, out_ref):
    width = out_ref.shape[1]
    out_ref[...] = jnp.dot(
        attended_ref[...],
        weight_ref[:, pl.ds(first_column(half, far, start, width), width)],
        preferred_element_type=jnp.float32,
    ).astype(jnp.bfloat16)


def project(attended, weight, half, far, start, width):
    depth = weight.shape[0]
    return pl.pallas_call(
        functools.partial(project_kernel, half, far, start),
        out_shape=jax.ShapeDtypeStruct((attended.shape[0], width), jnp.bfloat16),
        in_specs=[VMEM_SPEC, VMEM_SPEC],
        out_specs=VMEM_SPEC,
        compiler_params=PARAMS,
        cost_estimate=pl.CostEstimate(
            flops=2 * attended.shape[0] * depth * width, bytes_accessed=2 * depth * width, transcendentals=0
        ),
    )(attended, weight)


def add(a, b):
    return (a.astype(jnp.float32) + b.astype(jnp.float32)).astype(jnp.bfloat16)


def final_kernel(layout, *refs):
    out_ref = refs[-1]
    at = 0
    for kind, far, start, width in layout:
        if kind == "split":
            for half in (1, 0):
                out_ref[:, pl.ds(first_column(half, far, start, width // 2), width // 2)] = refs[at + 1 - half][...]
        else:
            out_ref[:, start : start + width] = add(refs[at][...], refs[at + 1][...])
        at += 2


def summed_over_four(attended, weight):
    columns = weight.shape[1]
    layout, start = [], 0
    for kind, far, eighths in PARTS:
        layout.append((kind, far, start, columns * eighths // 8))
        start += columns * eighths // 8
    first = {}
    got = {}
    for kind, far, start, width in layout:
        if kind == "split":
            got[start] = swapped(project(attended, weight, 0, far, start, width // 2), 1)
        else:
            first[start] = project(attended, weight, None, far, start, width)
            got[start] = swapped(first[start], 1 if kind == "near" else far)
    for kind, far, start, width in layout:
        if kind == "split":
            first[start] = project(attended, weight, 1, far, start, width // 2)
    operands = []
    for kind, far, start, width in layout:
        total = add(first[start], got[start])
        if kind == "split":
            total = add(total, swapped(total, far))
            operands += [total, swapped(total, 1)]
        else:
            operands += [total, swapped(total, far if kind == "near" else 1)]
    return pl.pallas_call(
        functools.partial(final_kernel, layout),
        out_shape=jax.ShapeDtypeStruct((attended.shape[0], columns), jnp.bfloat16),
        in_specs=[VMEM_SPEC] * len(operands),
        out_specs=VMEM_SPEC,
        compiler_params=PARAMS,
    )(*operands)


def summed_over_any(attended, weight):
    return lax.psum(project(attended, weight, None, 2, 0, weight.shape[1]), "mp")


def local(queries, prefix_pool, slot_offset, suffix_kv, out_weight):
    _, _, _, block, head_dim = prefix_pool.shape
    samples, _, _, length_of_suffix, _ = suffix_kv.shape
    local_heads = queries.shape[1] // head_dim
    rows = samples * local_heads
    f32, bf16 = jnp.float32, jnp.bfloat16
    queries_hbm, suffix = [pltpu.with_memory_space_constraint(x, pltpu.HBM) for x in (queries, suffix_kv)]
    mask = pl.pallas_call(
        functools.partial(mask_kernel, samples),
        out_shape=pltpu.VMEM((rows, samples * length_of_suffix), f32),
        out_specs=VMEM_SPEC,
        compiler_params=PARAMS,
        cost_estimate=lasting(8),
    )()
    length = CAPACITY * block
    gathered = pltpu.VMEM((1 + len(ASKED), length, head_dim), bf16)
    partial = (pltpu.VMEM((rows, head_dim), f32),) * 3
    asked = [shifted(queries, -lag) for lag in ASKED]
    keys, values, bias, *packs = pl.pallas_call(
        functools.partial(gather_kernel, local_heads),
        out_shape=(gathered, gathered, pltpu.VMEM((1 + len(ASKED), 8, length), f32))
        + (pltpu.VMEM((2 * length + CAPACITY * FLAG_ROWS, head_dim), bf16),) * len(SENT),
        in_specs=[VMEM_SPEC, pl.BlockSpec(memory_space=pltpu.SMEM), VMEM_SPEC],
        out_specs=(VMEM_SPEC,) * (3 + len(SENT)),
        compiler_params=PARAMS,
        cost_estimate=lasting(8),
    )(mask, slot_offset, prefix_pool)
    held = [shifted(pack, lag) for pack, lag in zip(packs, SENT)]
    answers = pl.pallas_call(
        lag_kernel,
        out_shape=(jax.ShapeDtypeStruct((rows + STAT_ROWS, head_dim), bf16),) * len(ASKED),
        in_specs=[VMEM_SPEC] * (3 + len(ASKED)),
        out_specs=(VMEM_SPEC,) * len(ASKED),
        compiler_params=PARAMS,
        cost_estimate=lasting(0.4),
    )(keys, values, bias, *asked)
    parts = [shifted(answer, lag) for answer, lag in zip(answers, ASKED)]
    own = pl.pallas_call(
        functools.partial(own_kernel, local_heads),
        out_shape=partial,
        in_specs=[VMEM_SPEC] * 5 + [HBM_SPEC] * 2,
        out_specs=(VMEM_SPEC,) * 3,
        scratch_shapes=[
            pltpu.VMEM(queries.shape, bf16),
            pltpu.VMEM((samples, 2, length_of_suffix, head_dim), bf16),
            pltpu.SemaphoreType.DMA((2,)),
        ],
        compiler_params=PARAMS,
        cost_estimate=lasting(1.6),
    )(keys, values, bias, mask, answers[-1], queries_hbm, suffix)
    others = pl.pallas_call(
        held_kernel,
        out_shape=partial,
        in_specs=[VMEM_SPEC] * (2 + len(SENT)),
        out_specs=(VMEM_SPEC,) * 3,
        compiler_params=PARAMS,
        cost_estimate=lasting(0.5),
    )(own[0], queries, *held)
    attended = pl.pallas_call(
        merge_kernel,
        out_shape=jax.ShapeDtypeStruct(queries.shape, bf16),
        in_specs=[VMEM_SPEC] * (6 + len(ASKED)),
        out_specs=VMEM_SPEC,
        compiler_params=PARAMS,
        cost_estimate=lasting(0.2),
    )(*own, *others, *parts)
    if lax.axis_size("mp") == 4:
        return summed_over_four(attended, out_weight)
    return summed_over_any(attended, out_weight)


def solution(mesh):
    placed = (
        P("dp", "mp"),
        P("dp", None, None, None, None),
        P("dp"),
        P("dp", None, None, None, None),
        P("mp", None),
    )
    return jax.shard_map(
        local, mesh=mesh, in_specs=placed, out_specs=P("dp", None), check_vma=False
    )
```

```python
import functools

import jax
import jax.numpy as jnp
from jax import lax
from jax.experimental import pallas as pl
from jax.experimental.pallas import tpu as pltpu
from jax.sharding import PartitionSpec as P

GQA = 8
SPREAD = 6
CAPACITY = 2
PARTS = (("split", 2, 4), ("near", 3, 4))
ASKED = (1, 2, 4)
SENT = (3, 5)
FLAG_ROWS = 8
STAT_ROWS = 16
NEG = -(2.0**100)

VMEM_SPEC = pl.BlockSpec(memory_space=pltpu.VMEM)
HBM_SPEC = pl.BlockSpec(memory_space=pltpu.HBM)
PARAMS = pltpu.CompilerParams(vmem_limit_bytes=16 * 1024 * 1024)


def lasting(us):
    return pl.CostEstimate(
        flops=int(us * 1.1e9), bytes_accessed=int(us * 3.69e6), transcendentals=int(us * 1e7)
    )


def shifted(block, distance):
    size = lax.axis_size("dp")
    return lax.ppermute(block, "dp", [(i, (i + distance) % size) for i in range(size)])


def swapped(block, step):
    size = lax.axis_size("mp")
    return lax.ppermute(block, "mp", [(i, i ^ step) for i in range(size)])


def head_rows(block, head_dim):
    heads = block.shape[1] // head_dim
    return jnp.concatenate([block[:, h * head_dim : (h + 1) * head_dim] for h in range(heads)], axis=0)


def dot_nt(a, b):
    return lax.dot_general(a, b, (((1,), (1,)), ((), ())), preferred_element_type=jnp.float32)


def slots_of(offset_ref, lag):
    first = jnp.int32(0)
    second = jnp.int32(0)
    count = jnp.int32(0)
    for b in range(offset_ref.shape[0]):
        hit = offset_ref[b] == lag
        second = jnp.where(hit & (count == 1), b, second)
        first = jnp.where(hit & (count == 0), b, first)
        count = count + hit.astype(jnp.int32)
    return (first, second), count


def first_column(half, far, start, width):
    if half is None:
        return start
    place = lax.axis_index("mp")
    kept = place % 2 if far == 2 else (place + place // 2) % 2
    return pl.multiple_of(start + (kept if half else 1 - kept) * width, 128)


def mask_kernel(samples, out_ref):
    rows, keys = out_ref.shape
    length = keys // samples
    row_sample = lax.broadcasted_iota(jnp.int32, (rows, keys), 0) % samples
    key_at = lax.broadcasted_iota(jnp.int32, (rows, keys), 1)
    mine = (key_at >= row_sample * length) & (key_at < (row_sample + 1) * length)
    out_ref[...] = jnp.where(mine, 0.0, NEG)


def gather_kernel(local_heads, after_ref, offset_ref, pool_ref, key_ref, value_ref, bias_ref, *refs):
    pack_refs = dict(zip(SENT, refs))
    kv = lax.axis_index("mp") * local_heads // GQA
    block, head_dim = pool_ref.shape[3:]
    found = [slots_of(offset_ref, lag) for lag in range(SPREAD)]
    at = lax.broadcasted_iota(jnp.int32, bias_ref.shape[1:], 1)
    kept = (0,) + ASKED
    for i, lag in enumerate(kept):
        bias_ref[i] = jnp.where(at < found[lag][1] * block, 0.0, NEG)
    at = lax.broadcasted_iota(jnp.int32, (2 * FLAG_ROWS, head_dim), 0)
    for lag, ref in pack_refs.items():
        ref[2 * CAPACITY * block :] = jnp.where(at < found[lag][1] * FLAG_ROWS, 0.0, NEG).astype(jnp.bfloat16)
    for lag, (slots, _) in enumerate(found):
        for position, slot in enumerate(slots):
            if lag in SENT:
                at = position * block
                pack_refs[lag][at : at + block] = pool_ref[slot, kv, 0]
                pack_refs[lag][CAPACITY * block + at : CAPACITY * block + at + block] = pool_ref[slot, kv, 1]
            else:
                place = slice(position * block, (position + 1) * block)
                key_ref[kept.index(lag), place] = pool_ref[slot, kv, 0]
                value_ref[kept.index(lag), place] = pool_ref[slot, kv, 1]


def held_kernel(after_ref, query_ref, *refs):
    pack_refs, (acc_ref, peak_ref, total_ref) = refs[: len(SENT)], refs[len(SENT) :]
    head_dim = pack_refs[0].shape[1]
    length = (pack_refs[0].shape[0] - CAPACITY * FLAG_ROWS) // 2
    block = length // CAPACITY
    scale = head_dim ** (-0.5)
    rows = head_rows(query_ref[...], head_dim)
    scores = []
    for ref in pack_refs:
        flags = ref[2 * length :].astype(jnp.float32)
        bias = jnp.concatenate([flags[i * FLAG_ROWS : i * FLAG_ROWS + 1] for i in range(CAPACITY)], axis=1)
        scores.append(dot_nt(rows, ref[:length]) * scale + bias)
    peak = functools.reduce(jnp.maximum, [jnp.max(x, axis=1, keepdims=True) for x in scores])
    weights = [jnp.exp(x - peak) for x in scores]
    total = sum(jnp.sum(w, axis=1, keepdims=True) for w in weights)
    acc_ref[...] = sum(
        jnp.dot(w.astype(jnp.bfloat16), ref[length : 2 * length], preferred_element_type=jnp.float32)
        for w, ref in zip(weights, pack_refs)
    )
    peak_ref[...] = jnp.broadcast_to(peak, peak_ref.shape)
    total_ref[...] = jnp.broadcast_to(total, total_ref.shape)


def diagonal(rows, lanes):
    shape = (rows, lanes)
    return lax.broadcasted_iota(jnp.int32, shape, 0) == lax.broadcasted_iota(jnp.int32, shape, 1)


def along_lanes(column, lanes):
    return jnp.sum(jnp.where(diagonal(column.shape[0], lanes), column, 0.0), axis=0, keepdims=True)


def along_rows(row, rows):
    return jnp.sum(jnp.where(diagonal(rows, row.shape[1]), row, 0.0), axis=1, keepdims=True)


def lag_kernel(key_ref, value_ref, bias_ref, *refs):
    query_refs, out_refs = refs[: len(ASKED)], refs[len(ASKED) :]
    lags = range(1, 1 + len(ASKED))
    head_dim = key_ref.shape[-1]
    scale = head_dim ** (-0.5)
    rows = [head_rows(ref[...], head_dim) for ref in query_refs]
    scores = [dot_nt(r, key_ref[lag]) * scale + bias_ref[lag][:1] for r, lag in zip(rows, lags)]
    peaks = [jnp.max(x, axis=1, keepdims=True).astype(jnp.bfloat16) for x in scores]
    weights = [jnp.exp(x - peak.astype(jnp.float32)) for x, peak in zip(scores, peaks)]
    accs = [
        jnp.dot(w.astype(jnp.bfloat16), value_ref[lag], preferred_element_type=jnp.float32)
        for w, lag in zip(weights, lags)
    ]
    totals = [jnp.sum(w, axis=1, keepdims=True).astype(jnp.bfloat16) for w in weights]
    length = rows[0].shape[0]
    at = lax.broadcasted_iota(jnp.int32, (STAT_ROWS, head_dim), 0)
    for out_ref, acc, peak, total in zip(out_refs, accs, peaks, totals):
        out_ref[:length] = acc.astype(jnp.bfloat16)
        laid = [along_lanes(x.astype(jnp.float32), head_dim) for x in (peak, total)]
        out_ref[length:] = jnp.where(at == 0, laid[0], jnp.where(at == 1, laid[1], 0.0)).astype(jnp.bfloat16)


def own_kernel(local_heads, key_ref, value_ref, bias_ref, mask_ref, after_ref, query_hbm, suffix_hbm,
               acc_ref, peak_ref, total_ref, query_ref, suffix_ref, sems):
    kv = lax.axis_index("mp") * local_heads // GQA
    samples, _, length, head_dim = suffix_ref.shape
    scale = head_dim ** (-0.5)
    copies = [
        pltpu.make_async_copy(query_hbm, query_ref, sems.at[0]),
        pltpu.make_async_copy(suffix_hbm.at[:, kv], suffix_ref, sems.at[1]),
    ]
    for copy in copies:
        copy.start()
    copies[0].wait()
    rows = head_rows(query_ref[...], head_dim)
    scores = dot_nt(rows, key_ref[0]) * scale + bias_ref[0][:1]
    copies[1].wait()
    suffix_keys = suffix_ref[:, 0].reshape(samples * length, head_dim)
    suffix_values = suffix_ref[:, 1].reshape(samples * length, head_dim)
    suffix_scores = dot_nt(rows, suffix_keys) * scale + mask_ref[...]
    peak = jnp.maximum(
        jnp.max(suffix_scores, axis=1, keepdims=True), jnp.max(scores, axis=1, keepdims=True)
    )
    suffix_weight = jnp.exp(suffix_scores - peak)
    weight = jnp.exp(scores - peak)
    total = jnp.sum(suffix_weight, axis=1, keepdims=True) + jnp.sum(weight, axis=1, keepdims=True)
    acc_ref[...] = jnp.dot(
        suffix_weight.astype(jnp.bfloat16), suffix_values, preferred_element_type=jnp.float32
    ) + jnp.dot(weight.astype(jnp.bfloat16), value_ref[0], preferred_element_type=jnp.float32)
    peak_ref[...] = jnp.broadcast_to(peak, peak_ref.shape)
    total_ref[...] = jnp.broadcast_to(total, total_ref.shape)


def merge_kernel(first, *refs):
    if first is not None:
        *refs, weight_ref, out_ref, sent_ref = refs
    else:
        *refs, out_ref = refs
    whole_refs, part_refs = refs[:6], refs[6:]
    rows, head_dim = whole_refs[0].shape
    samples = out_ref.shape[0]
    accs = [ref[...] for ref in whole_refs[0::3]]
    peaks = [ref[...][:, :1] for ref in whole_refs[1::3]]
    totals = [ref[...][:, :1] for ref in whole_refs[2::3]]
    for ref in part_refs:
        part = ref[...].astype(jnp.float32)
        accs.append(part[:rows])
        peaks.append(along_rows(part[rows : rows + 1], rows))
        totals.append(along_rows(part[rows + 1 : rows + 2], rows))
    top = functools.reduce(jnp.maximum, peaks)
    shares = [jnp.exp(peak - top) for peak in peaks]
    total = sum(share * t for share, t in zip(shares, totals))
    acc = sum(share * a for share, a in zip(shares, accs))
    attended = (acc / total).astype(jnp.bfloat16)
    attended = jnp.concatenate(
        [attended[h * samples : (h + 1) * samples] for h in range(rows // samples)], axis=1
    )
    out_ref[...] = attended
    if first is not None:
        width = sent_ref.shape[1]
        sent_ref[...] = jnp.dot(
            attended,
            weight_ref[:, pl.ds(first_column(*first, width), width)],
            preferred_element_type=jnp.float32,
        ).astype(jnp.bfloat16)


def project_kernel(half, far, start, attended_ref, weight_ref, out_ref):
    width = out_ref.shape[1]
    out_ref[...] = jnp.dot(
        attended_ref[...],
        weight_ref[:, pl.ds(first_column(half, far, start, width), width)],
        preferred_element_type=jnp.float32,
    ).astype(jnp.bfloat16)


def project(attended, weight, half, far, start, width):
    depth = weight.shape[0]
    return pl.pallas_call(
        functools.partial(project_kernel, half, far, start),
        out_shape=jax.ShapeDtypeStruct((attended.shape[0], width), jnp.bfloat16),
        in_specs=[VMEM_SPEC, VMEM_SPEC],
        out_specs=VMEM_SPEC,
        compiler_params=PARAMS,
        cost_estimate=pl.CostEstimate(
            flops=2 * attended.shape[0] * depth * width, bytes_accessed=2 * depth * width, transcendentals=0
        ),
    )(attended, weight)


def add(a, b):
    return (a.astype(jnp.float32) + b.astype(jnp.float32)).astype(jnp.bfloat16)


def final_kernel(layout, *refs):
    out_ref = refs[-1]
    at = 0
    for kind, far, start, width in layout:
        if kind == "split":
            for half in (1, 0):
                out_ref[:, pl.ds(first_column(half, far, start, width // 2), width // 2)] = refs[at + 1 - half][...]
        else:
            out_ref[:, start : start + width] = add(refs[at][...], refs[at + 1][...])
        at += 2


def summed_over_four(attended, sent, weight):
    columns = weight.shape[1]
    layout, start = [], 0
    for kind, far, eighths in PARTS:
        layout.append((kind, far, start, columns * eighths // 8))
        start += columns * eighths // 8
    first = {}
    got = {}
    for kind, far, start, width in layout:
        if kind == "split":
            got[start] = swapped(sent, 1)
        else:
            first[start] = project(attended, weight, None, far, start, width)
            got[start] = swapped(first[start], 1 if kind == "near" else far)
    for kind, far, start, width in layout:
        if kind == "split":
            first[start] = project(attended, weight, 1, far, start, width // 2)
    operands = []
    for kind, far, start, width in layout:
        total = add(first[start], got[start])
        if kind == "split":
            total = add(total, swapped(total, far))
            operands += [total, swapped(total, 1)]
        else:
            operands += [total, swapped(total, far if kind == "near" else 1)]
    return pl.pallas_call(
        functools.partial(final_kernel, layout),
        out_shape=jax.ShapeDtypeStruct((attended.shape[0], columns), jnp.bfloat16),
        in_specs=[VMEM_SPEC] * len(operands),
        out_specs=VMEM_SPEC,
        compiler_params=PARAMS,
    )(*operands)


def summed_over_any(attended, weight):
    return lax.psum(project(attended, weight, None, 2, 0, weight.shape[1]), "mp")


def local(queries, prefix_pool, slot_offset, suffix_kv, out_weight):
    _, _, _, block, head_dim = prefix_pool.shape
    samples, _, _, length_of_suffix, _ = suffix_kv.shape
    local_heads = queries.shape[1] // head_dim
    rows = samples * local_heads
    f32, bf16 = jnp.float32, jnp.bfloat16
    queries_hbm, suffix = [pltpu.with_memory_space_constraint(x, pltpu.HBM) for x in (queries, suffix_kv)]
    mask = pl.pallas_call(
        functools.partial(mask_kernel, samples),
        out_shape=pltpu.VMEM((rows, samples * length_of_suffix), f32),
        out_specs=VMEM_SPEC,
        compiler_params=PARAMS,
        cost_estimate=lasting(8),
    )()
    length = CAPACITY * block
    gathered = pltpu.VMEM((1 + len(ASKED), length, head_dim), bf16)
    partial = (pltpu.VMEM((rows, head_dim), f32),) * 3
    asked = [shifted(queries, -lag) for lag in ASKED]
    keys, values, bias, *packs = pl.pallas_call(
        functools.partial(gather_kernel, local_heads),
        out_shape=(gathered, gathered, pltpu.VMEM((1 + len(ASKED), 8, length), f32))
        + (pltpu.VMEM((2 * length + CAPACITY * FLAG_ROWS, head_dim), bf16),) * len(SENT),
        in_specs=[VMEM_SPEC, pl.BlockSpec(memory_space=pltpu.SMEM), VMEM_SPEC],
        out_specs=(VMEM_SPEC,) * (3 + len(SENT)),
        compiler_params=PARAMS,
        cost_estimate=lasting(8),
    )(mask, slot_offset, prefix_pool)
    held = [shifted(pack, lag) for pack, lag in zip(packs, SENT)]
    answers = pl.pallas_call(
        lag_kernel,
        out_shape=(jax.ShapeDtypeStruct((rows + STAT_ROWS, head_dim), bf16),) * len(ASKED),
        in_specs=[VMEM_SPEC] * (3 + len(ASKED)),
        out_specs=(VMEM_SPEC,) * len(ASKED),
        compiler_params=PARAMS,
        cost_estimate=lasting(0.4),
    )(keys, values, bias, *asked)
    parts = [shifted(answer, lag) for answer, lag in zip(answers, ASKED)]
    own = pl.pallas_call(
        functools.partial(own_kernel, local_heads),
        out_shape=partial,
        in_specs=[VMEM_SPEC] * 5 + [HBM_SPEC] * 2,
        out_specs=(VMEM_SPEC,) * 3,
        scratch_shapes=[
            pltpu.VMEM(queries.shape, bf16),
            pltpu.VMEM((samples, 2, length_of_suffix, head_dim), bf16),
            pltpu.SemaphoreType.DMA((2,)),
        ],
        compiler_params=PARAMS,
        cost_estimate=lasting(1.6),
    )(keys, values, bias, mask, answers[-1], queries_hbm, suffix)
    others = pl.pallas_call(
        held_kernel,
        out_shape=partial,
        in_specs=[VMEM_SPEC] * (2 + len(SENT)),
        out_specs=(VMEM_SPEC,) * 3,
        compiler_params=PARAMS,
        cost_estimate=lasting(0.5),
    )(own[0], queries, *held)
    four = lax.axis_size("mp") == 4
    (_, far, eighths), columns = PARTS[0], out_weight.shape[1]
    shapes = [jax.ShapeDtypeStruct(queries.shape, bf16)]
    if four:
        shapes.append(jax.ShapeDtypeStruct((samples, columns * eighths // 16), bf16))
    attended, *sent = pl.pallas_call(
        functools.partial(merge_kernel, (0, far, 0) if four else None),
        out_shape=tuple(shapes),
        in_specs=[VMEM_SPEC] * (6 + len(ASKED) + four),
        out_specs=(VMEM_SPEC,) * len(shapes),
        compiler_params=PARAMS,
        cost_estimate=lasting(0.2),
    )(*own, *others, *parts, *([out_weight] if four else []))
    if four:
        return summed_over_four(attended, sent[0], out_weight)
    return summed_over_any(attended, out_weight)


def solution(mesh):
    placed = (
        P("dp", "mp"),
        P("dp", None, None, None, None),
        P("dp"),
        P("dp", None, None, None, None),
        P("mp", None),
    )
    return jax.shard_map(
        local, mesh=mesh, in_specs=placed, out_specs=P("dp", None), check_vma=False
    )
```

```python
import functools

import jax
import jax.numpy as jnp
from jax import lax
from jax.experimental import pallas as pl
from jax.experimental.pallas import tpu as pltpu
from jax.sharding import PartitionSpec as P

GQA = 8
SPREAD = 6
CAPACITY = 2
PARTS = (("split", 2, 4), ("near", 3, 4))
ASKED = (1, 2, 4)
SENT = (3, 5)
FLAG_ROWS = 8
STAT_ROWS = 16
NEG = -(2.0**100)

VMEM_SPEC = pl.BlockSpec(memory_space=pltpu.VMEM)
HBM_SPEC = pl.BlockSpec(memory_space=pltpu.HBM)
PARAMS = pltpu.CompilerParams(vmem_limit_bytes=16 * 1024 * 1024)


def lasting(us):
    return pl.CostEstimate(
        flops=int(us * 1.1e9), bytes_accessed=int(us * 3.69e6), transcendentals=int(us * 1e7)
    )


def shifted(block, distance):
    size = lax.axis_size("dp")
    return lax.ppermute(block, "dp", [(i, (i + distance) % size) for i in range(size)])


def swapped(block, step):
    size = lax.axis_size("mp")
    return lax.ppermute(block, "mp", [(i, i ^ step) for i in range(size)])


def head_rows(block, head_dim):
    heads = block.shape[1] // head_dim
    return jnp.concatenate([block[:, h * head_dim : (h + 1) * head_dim] for h in range(heads)], axis=0)


def dot_nt(a, b):
    return lax.dot_general(a, b, (((1,), (1,)), ((), ())), preferred_element_type=jnp.float32)


def slots_of(offset_ref, lag):
    first = jnp.int32(0)
    second = jnp.int32(0)
    count = jnp.int32(0)
    for b in range(offset_ref.shape[0]):
        hit = offset_ref[b] == lag
        second = jnp.where(hit & (count == 1), b, second)
        first = jnp.where(hit & (count == 0), b, first)
        count = count + hit.astype(jnp.int32)
    return (first, second), count


def first_column(half, far, start, width):
    if half is None:
        return start
    place = lax.axis_index("mp")
    kept = place % 2 if far == 2 else (place + place // 2) % 2
    return pl.multiple_of(start + (kept if half else 1 - kept) * width, 128)


def mask_kernel(samples, out_ref):
    rows, keys = out_ref.shape
    length = keys // samples
    row_sample = lax.broadcasted_iota(jnp.int32, (rows, keys), 0) % samples
    key_at = lax.broadcasted_iota(jnp.int32, (rows, keys), 1)
    mine = (key_at >= row_sample * length) & (key_at < (row_sample + 1) * length)
    out_ref[...] = jnp.where(mine, 0.0, NEG)


def gather_kernel(local_heads, after_ref, offset_ref, pool_ref, key_ref, value_ref, bias_ref, *refs):
    pack_refs = dict(zip(SENT, refs))
    kv = lax.axis_index("mp") * local_heads // GQA
    block, head_dim = pool_ref.shape[3:]
    found = [slots_of(offset_ref, lag) for lag in range(SPREAD)]
    at = lax.broadcasted_iota(jnp.int32, bias_ref.shape[1:], 1)
    kept = (0,) + ASKED
    for i, lag in enumerate(kept):
        bias_ref[i] = jnp.where(at < found[lag][1] * block, 0.0, NEG)
    at = lax.broadcasted_iota(jnp.int32, (2 * FLAG_ROWS, head_dim), 0)
    for lag, ref in pack_refs.items():
        ref[2 * CAPACITY * block :] = jnp.where(at < found[lag][1] * FLAG_ROWS, 0.0, NEG).astype(jnp.bfloat16)
    for lag, (slots, _) in enumerate(found):
        for position, slot in enumerate(slots):
            if lag in SENT:
                at = position * block
                pack_refs[lag][at : at + block] = pool_ref[slot, kv, 0]
                pack_refs[lag][CAPACITY * block + at : CAPACITY * block + at + block] = pool_ref[slot, kv, 1]
            else:
                place = slice(position * block, (position + 1) * block)
                key_ref[kept.index(lag), place] = pool_ref[slot, kv, 0]
                value_ref[kept.index(lag), place] = pool_ref[slot, kv, 1]


def held_kernel(after_ref, query_ref, *refs):
    pack_refs, (acc_ref, peak_ref, total_ref) = refs[: len(SENT)], refs[len(SENT) :]
    head_dim = pack_refs[0].shape[1]
    length = (pack_refs[0].shape[0] - CAPACITY * FLAG_ROWS) // 2
    block = length // CAPACITY
    scale = head_dim ** (-0.5)
    rows = head_rows(query_ref[...], head_dim)
    scores = []
    for ref in pack_refs:
        flags = ref[2 * length :].astype(jnp.float32)
        bias = jnp.concatenate([flags[i * FLAG_ROWS : i * FLAG_ROWS + 1] for i in range(CAPACITY)], axis=1)
        scores.append(dot_nt(rows, ref[:length]) * scale + bias)
    peak = functools.reduce(jnp.maximum, [jnp.max(x, axis=1, keepdims=True) for x in scores])
    weights = [jnp.exp(x - peak) for x in scores]
    total = sum(jnp.sum(w, axis=1, keepdims=True) for w in weights)
    acc_ref[...] = sum(
        jnp.dot(w.astype(jnp.bfloat16), ref[length : 2 * length], preferred_element_type=jnp.float32)
        for w, ref in zip(weights, pack_refs)
    )
    peak_ref[...] = jnp.broadcast_to(peak, peak_ref.shape)
    total_ref[...] = jnp.broadcast_to(total, total_ref.shape)


def diagonal(rows, lanes):
    shape = (rows, lanes)
    return lax.broadcasted_iota(jnp.int32, shape, 0) == lax.broadcasted_iota(jnp.int32, shape, 1)


def along_lanes(column, lanes):
    return jnp.sum(jnp.where(diagonal(column.shape[0], lanes), column, 0.0), axis=0, keepdims=True)


def along_rows(row, rows):
    return jnp.sum(jnp.where(diagonal(rows, row.shape[1]), row, 0.0), axis=1, keepdims=True)


def lag_kernel(key_ref, value_ref, bias_ref, *refs):
    query_refs, out_refs = refs[: len(ASKED)], refs[len(ASKED) :]
    lags = range(1, 1 + len(ASKED))
    head_dim = key_ref.shape[-1]
    scale = head_dim ** (-0.5)
    rows = [head_rows(ref[...], head_dim) for ref in query_refs]
    scores = [dot_nt(r, key_ref[lag]) * scale + bias_ref[lag][:1] for r, lag in zip(rows, lags)]
    peaks = [jnp.max(x, axis=1, keepdims=True).astype(jnp.bfloat16) for x in scores]
    weights = [jnp.exp(x - peak.astype(jnp.float32)) for x, peak in zip(scores, peaks)]
    accs = [
        jnp.dot(w.astype(jnp.bfloat16), value_ref[lag], preferred_element_type=jnp.float32)
        for w, lag in zip(weights, lags)
    ]
    totals = [jnp.sum(w, axis=1, keepdims=True).astype(jnp.bfloat16) for w in weights]
    length = rows[0].shape[0]
    at = lax.broadcasted_iota(jnp.int32, (STAT_ROWS, head_dim), 0)
    for out_ref, acc, peak, total in zip(out_refs, accs, peaks, totals):
        out_ref[:length] = acc.astype(jnp.bfloat16)
        laid = [along_lanes(x.astype(jnp.float32), head_dim) for x in (peak, total)]
        out_ref[length:] = jnp.where(at == 0, laid[0], jnp.where(at == 1, laid[1], 0.0)).astype(jnp.bfloat16)


def own_kernel(local_heads, key_ref, value_ref, bias_ref, mask_ref, after_ref, query_hbm, suffix_hbm,
               acc_ref, peak_ref, total_ref, query_ref, suffix_ref, sems):
    kv = lax.axis_index("mp") * local_heads // GQA
    samples, _, length, head_dim = suffix_ref.shape
    scale = head_dim ** (-0.5)
    copies = [
        pltpu.make_async_copy(query_hbm, query_ref, sems.at[0]),
        pltpu.make_async_copy(suffix_hbm.at[:, kv], suffix_ref, sems.at[1]),
    ]
    for copy in copies:
        copy.start()
    copies[0].wait()
    rows = head_rows(query_ref[...], head_dim)
    scores = dot_nt(rows, key_ref[0]) * scale + bias_ref[0][:1]
    copies[1].wait()
    suffix_keys = suffix_ref[:, 0].reshape(samples * length, head_dim)
    suffix_values = suffix_ref[:, 1].reshape(samples * length, head_dim)
    suffix_scores = dot_nt(rows, suffix_keys) * scale + mask_ref[...]
    peak = jnp.maximum(
        jnp.max(suffix_scores, axis=1, keepdims=True), jnp.max(scores, axis=1, keepdims=True)
    )
    suffix_weight = jnp.exp(suffix_scores - peak)
    weight = jnp.exp(scores - peak)
    total = jnp.sum(suffix_weight, axis=1, keepdims=True) + jnp.sum(weight, axis=1, keepdims=True)
    acc_ref[...] = jnp.dot(
        suffix_weight.astype(jnp.bfloat16), suffix_values, preferred_element_type=jnp.float32
    ) + jnp.dot(weight.astype(jnp.bfloat16), value_ref[0], preferred_element_type=jnp.float32)
    peak_ref[...] = jnp.broadcast_to(peak, peak_ref.shape)
    total_ref[...] = jnp.broadcast_to(total, total_ref.shape)


def merge_kernel(first, *refs):
    if first is not None:
        *refs, weight_ref, out_ref, sent_ref = refs
    else:
        *refs, out_ref = refs
    whole_refs, part_refs = refs[:6], refs[6:]
    rows, head_dim = whole_refs[0].shape
    samples = out_ref.shape[0]
    accs = [ref[...] for ref in whole_refs[0::3]]
    peaks = [ref[...][:, :1] for ref in whole_refs[1::3]]
    totals = [ref[...][:, :1] for ref in whole_refs[2::3]]
    for ref in part_refs:
        part = ref[...].astype(jnp.float32)
        accs.append(part[:rows])
        stats = jnp.transpose(part[rows:])
        peaks.append(stats[:rows, 0:1])
        totals.append(stats[:rows, 1:2])
    top = functools.reduce(jnp.maximum, peaks)
    shares = [jnp.exp(peak - top) for peak in peaks]
    total = sum(share * t for share, t in zip(shares, totals))
    acc = sum(share * a for share, a in zip(shares, accs))
    attended = (acc / total).astype(jnp.bfloat16)
    attended = jnp.concatenate(
        [attended[h * samples : (h + 1) * samples] for h in range(rows // samples)], axis=1
    )
    out_ref[...] = attended
    if first is not None:
        width = sent_ref.shape[1]
        sent_ref[...] = jnp.dot(
            attended,
            weight_ref[:, pl.ds(first_column(*first, width), width)],
            preferred_element_type=jnp.float32,
        ).astype(jnp.bfloat16)


def project_kernel(half, far, start, attended_ref, weight_ref, out_ref):
    width = out_ref.shape[1]
    out_ref[...] = jnp.dot(
        attended_ref[...],
        weight_ref[:, pl.ds(first_column(half, far, start, width), width)],
        preferred_element_type=jnp.float32,
    ).astype(jnp.bfloat16)


def project(attended, weight, half, far, start, width):
    depth = weight.shape[0]
    return pl.pallas_call(
        functools.partial(project_kernel, half, far, start),
        out_shape=jax.ShapeDtypeStruct((attended.shape[0], width), jnp.bfloat16),
        in_specs=[VMEM_SPEC, VMEM_SPEC],
        out_specs=VMEM_SPEC,
        compiler_params=PARAMS,
        cost_estimate=pl.CostEstimate(
            flops=2 * attended.shape[0] * depth * width, bytes_accessed=2 * depth * width, transcendentals=0
        ),
    )(attended, weight)


def add(a, b):
    return (a.astype(jnp.float32) + b.astype(jnp.float32)).astype(jnp.bfloat16)


def final_kernel(layout, *refs):
    out_ref = refs[-1]
    at = 0
    for kind, far, start, width in layout:
        if kind == "split":
            for half in (1, 0):
                out_ref[:, pl.ds(first_column(half, far, start, width // 2), width // 2)] = refs[at + 1 - half][...]
        else:
            out_ref[:, start : start + width] = add(refs[at][...], refs[at + 1][...])
        at += 2


def summed_over_four(attended, sent, weight):
    columns = weight.shape[1]
    layout, start = [], 0
    for kind, far, eighths in PARTS:
        layout.append((kind, far, start, columns * eighths // 8))
        start += columns * eighths // 8
    first = {}
    got = {}
    for kind, far, start, width in layout:
        if kind == "split":
            got[start] = swapped(sent, 1)
        else:
            first[start] = project(attended, weight, None, far, start, width)
            got[start] = swapped(first[start], 1 if kind == "near" else far)
    for kind, far, start, width in layout:
        if kind == "split":
            first[start] = project(attended, weight, 1, far, start, width // 2)
    operands = []
    for kind, far, start, width in layout:
        total = add(first[start], got[start])
        if kind == "split":
            total = add(total, swapped(total, far))
            operands += [total, swapped(total, 1)]
        else:
            operands += [total, swapped(total, far if kind == "near" else 1)]
    return pl.pallas_call(
        functools.partial(final_kernel, layout),
        out_shape=jax.ShapeDtypeStruct((attended.shape[0], columns), jnp.bfloat16),
        in_specs=[VMEM_SPEC] * len(operands),
        out_specs=VMEM_SPEC,
        compiler_params=PARAMS,
    )(*operands)


def summed_over_any(attended, weight):
    return lax.psum(project(attended, weight, None, 2, 0, weight.shape[1]), "mp")


def local(queries, prefix_pool, slot_offset, suffix_kv, out_weight):
    _, _, _, block, head_dim = prefix_pool.shape
    samples, _, _, length_of_suffix, _ = suffix_kv.shape
    local_heads = queries.shape[1] // head_dim
    rows = samples * local_heads
    f32, bf16 = jnp.float32, jnp.bfloat16
    queries_hbm, suffix = [pltpu.with_memory_space_constraint(x, pltpu.HBM) for x in (queries, suffix_kv)]
    mask = pl.pallas_call(
        functools.partial(mask_kernel, samples),
        out_shape=pltpu.VMEM((rows, samples * length_of_suffix), f32),
        out_specs=VMEM_SPEC,
        compiler_params=PARAMS,
        cost_estimate=lasting(8),
    )()
    length = CAPACITY * block
    gathered = pltpu.VMEM((1 + len(ASKED), length, head_dim), bf16)
    partial = (pltpu.VMEM((rows, head_dim), f32),) * 3
    asked = [shifted(queries, -lag) for lag in ASKED]
    keys, values, bias, *packs = pl.pallas_call(
        functools.partial(gather_kernel, local_heads),
        out_shape=(gathered, gathered, pltpu.VMEM((1 + len(ASKED), 8, length), f32))
        + (pltpu.VMEM((2 * length + CAPACITY * FLAG_ROWS, head_dim), bf16),) * len(SENT),
        in_specs=[VMEM_SPEC, pl.BlockSpec(memory_space=pltpu.SMEM), VMEM_SPEC],
        out_specs=(VMEM_SPEC,) * (3 + len(SENT)),
        compiler_params=PARAMS,
        cost_estimate=lasting(8),
    )(mask, slot_offset, prefix_pool)
    held = [shifted(pack, lag) for pack, lag in zip(packs, SENT)]
    answers = pl.pallas_call(
        lag_kernel,
        out_shape=(jax.ShapeDtypeStruct((rows + STAT_ROWS, head_dim), bf16),) * len(ASKED),
        in_specs=[VMEM_SPEC] * (3 + len(ASKED)),
        out_specs=(VMEM_SPEC,) * len(ASKED),
        compiler_params=PARAMS,
        cost_estimate=lasting(0.4),
    )(keys, values, bias, *asked)
    parts = [shifted(answer, lag) for answer, lag in zip(answers, ASKED)]
    own = pl.pallas_call(
        functools.partial(own_kernel, local_heads),
        out_shape=partial,
        in_specs=[VMEM_SPEC] * 5 + [HBM_SPEC] * 2,
        out_specs=(VMEM_SPEC,) * 3,
        scratch_shapes=[
            pltpu.VMEM(queries.shape, bf16),
            pltpu.VMEM((samples, 2, length_of_suffix, head_dim), bf16),
            pltpu.SemaphoreType.DMA((2,)),
        ],
        compiler_params=PARAMS,
        cost_estimate=lasting(1.6),
    )(keys, values, bias, mask, answers[-1], queries_hbm, suffix)
    others = pl.pallas_call(
        held_kernel,
        out_shape=partial,
        in_specs=[VMEM_SPEC] * (2 + len(SENT)),
        out_specs=(VMEM_SPEC,) * 3,
        compiler_params=PARAMS,
        cost_estimate=lasting(0.5),
    )(own[0], queries, *held)
    four = lax.axis_size("mp") == 4
    (_, far, eighths), columns = PARTS[0], out_weight.shape[1]
    shapes = [jax.ShapeDtypeStruct(queries.shape, bf16)]
    if four:
        shapes.append(jax.ShapeDtypeStruct((samples, columns * eighths // 16), bf16))
    attended, *sent = pl.pallas_call(
        functools.partial(merge_kernel, (0, far, 0) if four else None),
        out_shape=tuple(shapes),
        in_specs=[VMEM_SPEC] * (6 + len(ASKED) + four),
        out_specs=(VMEM_SPEC,) * len(shapes),
        compiler_params=PARAMS,
        cost_estimate=lasting(0.2),
    )(*own, *others, *parts, *([out_weight] if four else []))
    if four:
        return summed_over_four(attended, sent[0], out_weight)
    return summed_over_any(attended, out_weight)


def solution(mesh):
    placed = (
        P("dp", "mp"),
        P("dp", None, None, None, None),
        P("dp"),
        P("dp", None, None, None, None),
        P("mp", None),
    )
    return jax.shard_map(
        local, mesh=mesh, in_specs=placed, out_specs=P("dp", None), check_vma=False
    )
```

```python
import functools

import jax
import jax.numpy as jnp
from jax import lax
from jax.experimental import pallas as pl
from jax.experimental.pallas import tpu as pltpu
from jax.sharding import PartitionSpec as P

GQA = 8
SPREAD = 6
CAPACITY = 2
PARTS = (("split", 2, 4), ("near", 3, 4))
ASKED = (1, 2, 4)
SENT = (3, 5)
FLAG_ROWS = 8
STAT_ROWS = 16
NEG = -(2.0**100)

VMEM_SPEC = pl.BlockSpec(memory_space=pltpu.VMEM)
HBM_SPEC = pl.BlockSpec(memory_space=pltpu.HBM)
PARAMS = pltpu.CompilerParams(vmem_limit_bytes=16 * 1024 * 1024)


def lasting(us):
    return pl.CostEstimate(
        flops=int(us * 1.1e9), bytes_accessed=int(us * 3.69e6), transcendentals=int(us * 1e7)
    )


def shifted(block, distance):
    size = lax.axis_size("dp")
    return lax.ppermute(block, "dp", [(i, (i + distance) % size) for i in range(size)])


def swapped(block, step):
    size = lax.axis_size("mp")
    return lax.ppermute(block, "mp", [(i, i ^ step) for i in range(size)])


def head_rows(block, head_dim):
    heads = block.shape[1] // head_dim
    return jnp.concatenate([block[:, h * head_dim : (h + 1) * head_dim] for h in range(heads)], axis=0)


def dot_nt(a, b):
    return lax.dot_general(a, b, (((1,), (1,)), ((), ())), preferred_element_type=jnp.float32)


def slots_of(offset_ref, lag):
    first = jnp.int32(0)
    second = jnp.int32(0)
    count = jnp.int32(0)
    for b in range(offset_ref.shape[0]):
        hit = offset_ref[b] == lag
        second = jnp.where(hit & (count == 1), b, second)
        first = jnp.where(hit & (count == 0), b, first)
        count = count + hit.astype(jnp.int32)
    return (first, second), count


def first_column(half, far, start, width):
    if half is None:
        return start
    place = lax.axis_index("mp")
    kept = place % 2 if far == 2 else (place + place // 2) % 2
    return pl.multiple_of(start + (kept if half else 1 - kept) * width, 128)


def mask_kernel(samples, out_ref):
    rows, keys = out_ref.shape
    length = keys // samples
    row_sample = lax.broadcasted_iota(jnp.int32, (rows, keys), 0) % samples
    key_at = lax.broadcasted_iota(jnp.int32, (rows, keys), 1)
    mine = (key_at >= row_sample * length) & (key_at < (row_sample + 1) * length)
    out_ref[...] = jnp.where(mine, 0.0, NEG)


def gather_kernel(local_heads, after_ref, offset_ref, pool_ref, key_ref, value_ref, bias_ref, *refs):
    pack_refs = dict(zip(SENT, refs))
    kv = lax.axis_index("mp") * local_heads // GQA
    block, head_dim = pool_ref.shape[3:]
    found = [slots_of(offset_ref, lag) for lag in range(SPREAD)]
    at = lax.broadcasted_iota(jnp.int32, bias_ref.shape[1:], 1)
    kept = (0,) + ASKED
    for i, lag in enumerate(kept):
        bias_ref[i] = jnp.where(at < found[lag][1] * block, 0.0, NEG)
    at = lax.broadcasted_iota(jnp.int32, (2 * FLAG_ROWS, head_dim), 0)
    for lag, ref in pack_refs.items():
        ref[2 * CAPACITY * block :] = jnp.where(at < found[lag][1] * FLAG_ROWS, 0.0, NEG).astype(jnp.bfloat16)
    for lag, (slots, _) in enumerate(found):
        for position, slot in enumerate(slots):
            if lag in SENT:
                at = position * block
                pack_refs[lag][at : at + block] = pool_ref[slot, kv, 0]
                pack_refs[lag][CAPACITY * block + at : CAPACITY * block + at + block] = pool_ref[slot, kv, 1]
            else:
                place = slice(position * block, (position + 1) * block)
                key_ref[kept.index(lag), place] = pool_ref[slot, kv, 0]
                value_ref[kept.index(lag), place] = pool_ref[slot, kv, 1]


def held_kernel(after_ref, query_ref, *refs):
    pack_refs, (acc_ref, peak_ref, total_ref) = refs[: len(SENT)], refs[len(SENT) :]
    head_dim = pack_refs[0].shape[1]
    length = (pack_refs[0].shape[0] - CAPACITY * FLAG_ROWS) // 2
    block = length // CAPACITY
    scale = head_dim ** (-0.5)
    rows = head_rows(query_ref[...], head_dim)
    scores = []
    for ref in pack_refs:
        flags = ref[2 * length :].astype(jnp.float32)
        bias = jnp.concatenate([flags[i * FLAG_ROWS : i * FLAG_ROWS + 1] for i in range(CAPACITY)], axis=1)
        scores.append(dot_nt(rows, ref[:length]) * scale + bias)
    peak = functools.reduce(jnp.maximum, [jnp.max(x, axis=1, keepdims=True) for x in scores])
    weights = [jnp.exp(x - peak) for x in scores]
    total = sum(jnp.sum(w, axis=1, keepdims=True) for w in weights)
    acc_ref[...] = sum(
        jnp.dot(w.astype(jnp.bfloat16), ref[length : 2 * length], preferred_element_type=jnp.float32)
        for w, ref in zip(weights, pack_refs)
    )
    peak_ref[...] = jnp.broadcast_to(peak, peak_ref.shape)
    total_ref[...] = jnp.broadcast_to(total, total_ref.shape)


def diagonal(rows, lanes):
    shape = (rows, lanes)
    return lax.broadcasted_iota(jnp.int32, shape, 0) == lax.broadcasted_iota(jnp.int32, shape, 1)


def along_lanes(column, lanes):
    return jnp.sum(jnp.where(diagonal(column.shape[0], lanes), column, 0.0), axis=0, keepdims=True)


def along_rows(row, rows):
    return jnp.sum(jnp.where(diagonal(rows, row.shape[1]), row, 0.0), axis=1, keepdims=True)


def lag_kernel(key_ref, value_ref, bias_ref, *refs):
    query_refs, out_refs = refs[: len(ASKED)], refs[len(ASKED) :]
    lags = range(1, 1 + len(ASKED))
    head_dim = key_ref.shape[-1]
    scale = head_dim ** (-0.5)
    rows = [head_rows(ref[...], head_dim) for ref in query_refs]
    scores = [dot_nt(r, key_ref[lag]) * scale + bias_ref[lag][:1] for r, lag in zip(rows, lags)]
    peaks = [jnp.max(x, axis=1, keepdims=True).astype(jnp.bfloat16) for x in scores]
    weights = [jnp.exp(x - peak.astype(jnp.float32)) for x, peak in zip(scores, peaks)]
    accs = [
        jnp.dot(w.astype(jnp.bfloat16), value_ref[lag], preferred_element_type=jnp.float32)
        for w, lag in zip(weights, lags)
    ]
    totals = [jnp.sum(w, axis=1, keepdims=True).astype(jnp.bfloat16) for w in weights]
    length = rows[0].shape[0]
    at = lax.broadcasted_iota(jnp.int32, (STAT_ROWS, head_dim), 0)
    for out_ref, acc, peak, total in zip(out_refs, accs, peaks, totals):
        out_ref[:length] = acc.astype(jnp.bfloat16)
        laid = [along_lanes(x.astype(jnp.float32), head_dim) for x in (peak, total)]
        out_ref[length:] = jnp.where(at == 0, laid[0], jnp.where(at == 1, laid[1], 0.0)).astype(jnp.bfloat16)


def own_kernel(local_heads, key_ref, value_ref, bias_ref, mask_ref, after_ref, query_hbm, suffix_hbm,
               acc_ref, peak_ref, total_ref, query_ref, suffix_ref, sems):
    kv = lax.axis_index("mp") * local_heads // GQA
    samples, _, length, head_dim = suffix_ref.shape
    scale = head_dim ** (-0.5)
    copies = [
        pltpu.make_async_copy(query_hbm, query_ref, sems.at[0]),
        pltpu.make_async_copy(suffix_hbm.at[:, kv], suffix_ref, sems.at[1]),
    ]
    for copy in copies:
        copy.start()
    copies[0].wait()
    rows = head_rows(query_ref[...], head_dim)
    scores = dot_nt(rows, key_ref[0]) * scale + bias_ref[0][:1]
    copies[1].wait()
    suffix_keys = suffix_ref[:, 0].reshape(samples * length, head_dim)
    suffix_values = suffix_ref[:, 1].reshape(samples * length, head_dim)
    suffix_scores = dot_nt(rows, suffix_keys) * scale + mask_ref[...]
    peak = jnp.maximum(
        jnp.max(suffix_scores, axis=1, keepdims=True), jnp.max(scores, axis=1, keepdims=True)
    )
    suffix_weight = jnp.exp(suffix_scores - peak)
    weight = jnp.exp(scores - peak)
    total = jnp.sum(suffix_weight, axis=1, keepdims=True) + jnp.sum(weight, axis=1, keepdims=True)
    acc_ref[...] = jnp.dot(
        suffix_weight.astype(jnp.bfloat16), suffix_values, preferred_element_type=jnp.float32
    ) + jnp.dot(weight.astype(jnp.bfloat16), value_ref[0], preferred_element_type=jnp.float32)
    peak_ref[...] = jnp.broadcast_to(peak, peak_ref.shape)
    total_ref[...] = jnp.broadcast_to(total, total_ref.shape)


def merge_kernel(first, *refs):
    if first is not None:
        *refs, weight_ref, out_ref, sent_ref = refs
    else:
        *refs, out_ref = refs
    whole_refs, part_refs = refs[:6], refs[6:]
    rows, head_dim = whole_refs[0].shape
    samples = out_ref.shape[0]
    accs = [ref[...] for ref in whole_refs[0::3]]
    peaks = [ref[...][:, :1] for ref in whole_refs[1::3]]
    totals = [ref[...][:, :1] for ref in whole_refs[2::3]]
    for ref in part_refs:
        part = ref[...].astype(jnp.float32)
        accs.append(part[:rows])
        peaks.append(along_rows(part[rows : rows + 1], rows))
        totals.append(along_rows(part[rows + 1 : rows + 2], rows))
    top = functools.reduce(jnp.maximum, peaks)
    shares = [jnp.exp(peak - top) for peak in peaks]
    total = sum(share * t for share, t in zip(shares, totals))
    acc = sum(share * a for share, a in zip(shares, accs))
    attended = (acc / total).astype(jnp.bfloat16)
    attended = jnp.concatenate(
        [attended[h * samples : (h + 1) * samples] for h in range(rows // samples)], axis=1
    )
    out_ref[...] = attended
    if first is not None:
        width = sent_ref.shape[1]
        sent_ref[...] = jnp.dot(
            attended,
            weight_ref[:, pl.ds(first_column(*first, width), width)],
            preferred_element_type=jnp.float32,
        ).astype(jnp.bfloat16)


def project_kernel(half, far, start, attended_ref, weight_ref, out_ref):
    width = out_ref.shape[1]
    out_ref[...] = jnp.dot(
        attended_ref[...],
        weight_ref[:, pl.ds(first_column(half, far, start, width), width)],
        preferred_element_type=jnp.float32,
    ).astype(jnp.bfloat16)


def project(attended, weight, half, far, start, width):
    depth = weight.shape[0]
    return pl.pallas_call(
        functools.partial(project_kernel, half, far, start),
        out_shape=jax.ShapeDtypeStruct((attended.shape[0], width), jnp.bfloat16),
        in_specs=[VMEM_SPEC, VMEM_SPEC],
        out_specs=VMEM_SPEC,
        compiler_params=PARAMS,
        cost_estimate=pl.CostEstimate(
            flops=2 * attended.shape[0] * depth * width, bytes_accessed=2 * depth * width, transcendentals=0
        ),
    )(attended, weight)


def add(a, b):
    return (a.astype(jnp.float32) + b.astype(jnp.float32)).astype(jnp.bfloat16)


def final_kernel(layout, *refs):
    *part_refs, out_hbm, sum_ref, sems = refs
    copies = []

    def send(ref, start):
        copies.append(
            pltpu.make_async_copy(ref, out_hbm.at[:, pl.ds(start, ref.shape[1])], sems.at[len(copies)])
        )
        copies[-1].start()

    at = 0
    for kind, far, start, width in layout:
        if kind == "split":
            for half in (1, 0):
                send(part_refs[at + 1 - half], first_column(half, far, start, width // 2))
        at += 2
    at = place = 0
    for kind, far, start, width in layout:
        if kind != "split":
            piece = sum_ref.at[:, place : place + width]
            piece[...] = add(part_refs[at][...], part_refs[at + 1][...])
            send(piece, start)
            place += width
        at += 2
    for copy in copies:
        copy.wait()


def summed_over_four(attended, sent, weight):
    columns = weight.shape[1]
    layout, start = [], 0
    for kind, far, eighths in PARTS:
        layout.append((kind, far, start, columns * eighths // 8))
        start += columns * eighths // 8
    first = {}
    got = {}
    for kind, far, start, width in layout:
        if kind == "split":
            got[start] = swapped(sent, 1)
        else:
            first[start] = project(attended, weight, None, far, start, width)
            got[start] = swapped(first[start], 1 if kind == "near" else far)
    for kind, far, start, width in layout:
        if kind == "split":
            first[start] = project(attended, weight, 1, far, start, width // 2)
    operands = []
    for kind, far, start, width in layout:
        total = add(first[start], got[start])
        if kind == "split":
            total = add(total, swapped(total, far))
            operands += [total, swapped(total, 1)]
        else:
            operands += [total, swapped(total, far if kind == "near" else 1)]
    return pl.pallas_call(
        functools.partial(final_kernel, layout),
        out_shape=jax.ShapeDtypeStruct((attended.shape[0], columns), jnp.bfloat16),
        in_specs=[VMEM_SPEC] * len(operands),
        out_specs=HBM_SPEC,
        scratch_shapes=[
            pltpu.VMEM((attended.shape[0], sum(w for kind, _, _, w in layout if kind != "split")), jnp.bfloat16),
            pltpu.SemaphoreType.DMA((2 * len(layout),)),
        ],
        compiler_params=PARAMS,
    )(*operands)


def summed_over_any(attended, weight):
    return lax.psum(project(attended, weight, None, 2, 0, weight.shape[1]), "mp")


def local(queries, prefix_pool, slot_offset, suffix_kv, out_weight):
    _, _, _, block, head_dim = prefix_pool.shape
    samples, _, _, length_of_suffix, _ = suffix_kv.shape
    local_heads = queries.shape[1] // head_dim
    rows = samples * local_heads
    f32, bf16 = jnp.float32, jnp.bfloat16
    queries_hbm, suffix = [pltpu.with_memory_space_constraint(x, pltpu.HBM) for x in (queries, suffix_kv)]
    mask = pl.pallas_call(
        functools.partial(mask_kernel, samples),
        out_shape=pltpu.VMEM((rows, samples * length_of_suffix), f32),
        out_specs=VMEM_SPEC,
        compiler_params=PARAMS,
        cost_estimate=lasting(8),
    )()
    length = CAPACITY * block
    gathered = pltpu.VMEM((1 + len(ASKED), length, head_dim), bf16)
    partial = (pltpu.VMEM((rows, head_dim), f32),) * 3
    asked = [shifted(queries, -lag) for lag in ASKED]
    keys, values, bias, *packs = pl.pallas_call(
        functools.partial(gather_kernel, local_heads),
        out_shape=(gathered, gathered, pltpu.VMEM((1 + len(ASKED), 8, length), f32))
        + (pltpu.VMEM((2 * length + CAPACITY * FLAG_ROWS, head_dim), bf16),) * len(SENT),
        in_specs=[VMEM_SPEC, pl.BlockSpec(memory_space=pltpu.SMEM), VMEM_SPEC],
        out_specs=(VMEM_SPEC,) * (3 + len(SENT)),
        compiler_params=PARAMS,
        cost_estimate=lasting(8),
    )(mask, slot_offset, prefix_pool)
    held = [shifted(pack, lag) for pack, lag in zip(packs, SENT)]
    answers = pl.pallas_call(
        lag_kernel,
        out_shape=(jax.ShapeDtypeStruct((rows + STAT_ROWS, head_dim), bf16),) * len(ASKED),
        in_specs=[VMEM_SPEC] * (3 + len(ASKED)),
        out_specs=(VMEM_SPEC,) * len(ASKED),
        compiler_params=PARAMS,
        cost_estimate=lasting(0.4),
    )(keys, values, bias, *asked)
    parts = [shifted(answer, lag) for answer, lag in zip(answers, ASKED)]
    own = pl.pallas_call(
        functools.partial(own_kernel, local_heads),
        out_shape=partial,
        in_specs=[VMEM_SPEC] * 5 + [HBM_SPEC] * 2,
        out_specs=(VMEM_SPEC,) * 3,
        scratch_shapes=[
            pltpu.VMEM(queries.shape, bf16),
            pltpu.VMEM((samples, 2, length_of_suffix, head_dim), bf16),
            pltpu.SemaphoreType.DMA((2,)),
        ],
        compiler_params=PARAMS,
        cost_estimate=lasting(1.6),
    )(keys, values, bias, mask, answers[-1], queries_hbm, suffix)
    others = pl.pallas_call(
        held_kernel,
        out_shape=partial,
        in_specs=[VMEM_SPEC] * (2 + len(SENT)),
        out_specs=(VMEM_SPEC,) * 3,
        compiler_params=PARAMS,
        cost_estimate=lasting(0.5),
    )(own[0], queries, *held)
    four = lax.axis_size("mp") == 4
    (_, far, eighths), columns = PARTS[0], out_weight.shape[1]
    shapes = [jax.ShapeDtypeStruct(queries.shape, bf16)]
    if four:
        shapes.append(jax.ShapeDtypeStruct((samples, columns * eighths // 16), bf16))
    attended, *sent = pl.pallas_call(
        functools.partial(merge_kernel, (0, far, 0) if four else None),
        out_shape=tuple(shapes),
        in_specs=[VMEM_SPEC] * (6 + len(ASKED) + four),
        out_specs=(VMEM_SPEC,) * len(shapes),
        compiler_params=PARAMS,
        cost_estimate=lasting(0.2),
    )(*own, *others, *parts, *([out_weight] if four else []))
    if four:
        return summed_over_four(attended, sent[0], out_weight)
    return summed_over_any(attended, out_weight)


def solution(mesh):
    placed = (
        P("dp", "mp"),
        P("dp", None, None, None, None),
        P("dp"),
        P("dp", None, None, None, None),
        P("mp", None),
    )
    return jax.shard_map(
        local, mesh=mesh, in_specs=placed, out_specs=P("dp", None), check_vma=False
    )
```
